256 devices in a mesh: member: 32 (over y, x, core), head: 8 (over z).
Axes of the slice: x: 4, y: 4, z: 8, core: 2. Of those that a mesh axis runs over, the one named last changes fastest.
Arguments:
- hidden: bfloat16 [32, 32, 16, 2880], P('member', 'head'), may hold values from -6 to 6
- joined_weight: bfloat16 [2880, 8, 640], P(None, 'head'), may hold values from -0.109375 to 0.109375
- output_weight: bfloat16 [4096, 2880], P('head'), may hold values from -0.09375 to 0.09375
- key_cache: bfloat16 [32, 8, 16, 65536], P('member', 'head'), may hold values from -330 to 330
- value_cache: bfloat16 [32, 8, 16, 65536], P('member', 'head'), may hold values from -8 to 8
- sink_logits: float32 [64], P('head'), may hold values from 3 to 10
- lengths: int32 [32, 16], P('member'), may hold values from 2 to 1024, as said below
- query_left: float32 [32, 4, 2880], P('member'), may hold values from -6 to 6
- query_right: float32 [32, 4, 4096], P('member', None, 'head'), may hold values from -6 to 6
- output_left: float32 [32, 4, 4096], P('member', None, 'head'), may hold values from -6 to 6
- output_right: float32 [32, 4, 2880], P('member'), may hold values from -6 to 6
- fitness: float32 [32], P('member'), may hold values from -4 to 4
- query_master: float32 [2880, 4096], P('member', 'head'), may hold values from -6 to 6
- query_moment: float32 [2880, 4096], P('member', 'head'), may hold values from -2 to 2
- output_master: float32 [2880, 4096], P('member', 'head'), may hold values from -6 to 6
- output_moment: float32 [2880, 4096], P('member', 'head'), may hold values from -2 to 2
Outputs:
- layer_output: bfloat16 [32, 32, 16, 2880], P('member', 'head')
- query_weights: float32 [2880, 4096], P('member', 'head')
- query_momenta: float32 [2880, 4096], P('member', 'head')
- output_weights: float32 [2880, 4096], P('member', 'head')
- output_momenta: float32 [2880, 4096], P('member', 'head')
The draws below stay inside these ranges and needn't reach their ends.
Inputs may be any that keep to these rules, and one draw needn't show every extreme that they name: `lengths`: in every member one sequence has all 1024 slots filled.
All inputs are finite; a program needn't handle non-finite values.
Results may differ from the reference program's by a relative error of at most 0.012.
Values may be sent and summed in bfloat16 or wider, within the bound.
No kernel may reach another device: no remote copies, remote signals or barrier semaphores. Data moves between devices by JAX's collectives and lax.ppermute only.
A program may use at most 128 MiB of HBM per device.

```python
import math
import jax
import jax.numpy as jnp
from jax import lax

D = 2880
HEADS = 64
KV_HEADS = 8
HEAD_DIM = 64
RANK = 4
ROWS = 16
CACHE = 1024
STEPS = 32
GROUP = 8
QDIM = 4096
MEMBERS = 32


def draw_key_cache(key, part):
    full_shape = (MEMBERS, KV_HEADS, ROWS, CACHE, HEAD_DIM)
    first_key = jax.random.fold_in(jax.random.fold_in(key, 11), 0)
    base_keys = 1.5 * jax.random.truncated_normal(first_key, -4.0, 4.0, full_shape, jnp.float32)
    return base_keys.reshape(MEMBERS, KV_HEADS, ROWS, CACHE * HEAD_DIM).astype(jnp.bfloat16)


def draw_lengths(key, part):
    first_key, second_key = jax.random.split(jax.random.fold_in(key, 23))
    drawn = jax.random.randint(first_key, (MEMBERS, ROWS), 2, CACHE + 1)
    full_row = jax.random.randint(second_key, (MEMBERS, 1), 0, ROWS)
    row_ids = jnp.arange(ROWS, dtype=jnp.int32)[None, :]
    return jnp.where(row_ids == full_row, CACHE, drawn).astype(jnp.int32)


def levels(key, dims, shards, least, largest):
    factor_of = 1.0
    for position, blocks in shards:
        draws = jax.random.uniform(jax.random.fold_in(jax.random.fold_in(key, 6), position), (blocks,), jnp.float32, least / len(shards), largest / len(shards))
        factor_of = factor_of * jnp.repeat(jnp.exp(draws), dims[position] // blocks).reshape((-1,) + (1,) * (len(dims) - 1 - position))
    return factor_of


def scatter_about(rng, shape, scale, limit, pieces=(), held_as=jnp.bfloat16):
    values = jax.random.normal(rng, shape, jnp.float32) * scale
    if len(pieces) > 0:
        values = levels(rng, shape, pieces, -0.22, 0.18) * values
    return jnp.clip(values, min=-limit, max=limit).astype(held_as)


def setup_inputs(seed: int = 0) -> dict:
    splits = jax.random.split(jax.random.key(seed), 17)
    hidden = scatter_about(splits[0], (MEMBERS, STEPS, ROWS, D), 1.0, 6.0, ((0, 32), (1, 8)))
    joined_weight = scatter_about(splits[1], (D, KV_HEADS, (GROUP + 2) * HEAD_DIM), D ** -0.5, 0.109375, ((1, 8),))
    output_weight = scatter_about(splits[2], (QDIM, D), QDIM ** -0.5, 0.09375, ((0, 8),))
    key_cache = draw_key_cache(jax.random.fold_in(splits[16], 71), 0)
    value_cache = scatter_about(splits[4], (MEMBERS, KV_HEADS, ROWS, CACHE * HEAD_DIM), 2.0, 8.0, ((0, 32), (1, 8)))
    sink_logits = jnp.clip(3.0 + 7.0 * jax.random.uniform(splits[5], (HEADS,), jnp.float32) ** levels(splits[5], (HEADS,), ((0, 8),), -0.2, 0.2), 3.0, 10.0)
    lengths = draw_lengths(jax.random.fold_in(splits[16], 71), 0)
    query_left = scatter_about(splits[7], (MEMBERS, RANK, D), 1.0, 6.0, ((0, 32),), jnp.float32)
    query_right = scatter_about(splits[8], (MEMBERS, RANK, QDIM), 1.0, 6.0, ((0, 32), (2, 8)), jnp.float32)
    output_left = scatter_about(splits[9], (MEMBERS, RANK, QDIM), 1.0, 6.0, ((0, 32), (2, 8)), jnp.float32)
    output_right = scatter_about(splits[10], (MEMBERS, RANK, D), 1.0, 6.0, ((0, 32),), jnp.float32)
    fitness = scatter_about(splits[11], (MEMBERS,), 1.0, 4.0, ((0, 32),), jnp.float32)
    query_master = scatter_about(splits[12], (D, QDIM), 1.0, 6.0, ((0, 32), (1, 8)), jnp.float32)
    query_moment = scatter_about(splits[13], (D, QDIM), 0.3, 2.0, ((0, 32), (1, 8)), jnp.float32)
    output_master = scatter_about(splits[14], (D, QDIM), 1.0, 6.0, ((0, 32), (1, 8)), jnp.float32)
    output_moment = scatter_about(splits[15], (D, QDIM), 0.3, 2.0, ((0, 32), (1, 8)), jnp.float32)
    return dict(hidden=hidden, joined_weight=joined_weight, output_weight=output_weight, key_cache=key_cache, value_cache=value_cache, sink_logits=sink_logits, lengths=lengths, query_left=query_left, query_right=query_right, output_left=output_left, output_right=output_right, fitness=fitness, query_master=query_master, query_moment=query_moment, output_master=output_master, output_moment=output_moment)


rotary_base = 150000.0
noise_scale = 0.5
moment_decay = 0.9
learn_rate = 0.2
masked_score = -1e+30

def rotate(vectors, positions):
    half_dim = vectors.shape[-1] // 2
    exponents = jnp.arange(half_dim, dtype=jnp.float32) * (-2.0 / vectors.shape[-1])
    frequency = jnp.power(jnp.float32(rotary_base), exponents)
    angles = positions.astype(jnp.float32)[..., None] * frequency
    cosines = jnp.cos(angles)
    sine_part = jnp.sin(angles)
    first_half = vectors[..., :half_dim]
    second_half = vectors[..., half_dim:]
    return jnp.concatenate([first_half * cosines - second_half * sine_part, second_half * cosines + first_half * sine_part], axis=-1)

def attend(projected, member_lengths, member_keys, member_values, sink_values):
    step_count, row_count, kv_count, width, head_dim = projected.shape
    group = width - 2
    cache_len = member_keys.shape[-1] // head_dim
    positions = member_lengths[None, :] + jnp.arange(step_count, dtype=jnp.int32)[:, None]
    queries = rotate(projected[:, :, :, :group], positions[:, :, None, None]).astype(jnp.bfloat16)
    keys_new = rotate(projected[:, :, :, group], positions[:, :, None]).astype(jnp.bfloat16)
    values_new = projected[:, :, :, group + 1].astype(jnp.bfloat16)
    cache_keys = member_keys.reshape(kv_count, row_count, cache_len, head_dim)
    cache_values = member_values.reshape(kv_count, row_count, cache_len, head_dim)
    score_scale = head_dim ** (-0.5)
    cache_scores = jnp.einsum('sbjgd,jbtd->jbgst', queries.astype(jnp.float32), cache_keys.astype(jnp.float32)) * score_scale
    in_cache = jnp.arange(cache_len, dtype=jnp.int32)[None, :] < member_lengths[:, None]
    cache_scores = jnp.where(in_cache[None, :, None, None, :], cache_scores, masked_score)
    new_scores = jnp.einsum('sbjgd,ubjd->jbgsu', queries.astype(jnp.float32), keys_new.astype(jnp.float32)) * score_scale
    earlier = jnp.arange(step_count)[None, :] <= jnp.arange(step_count)[:, None]
    new_scores = jnp.where(earlier[None, None, None, :, :], new_scores, masked_score)
    sinks = sink_values.reshape(kv_count, 1, group, 1)
    maximum = jnp.maximum(jnp.maximum(cache_scores.max(-1), new_scores.max(-1)), sinks)
    cache_exp = jnp.exp(cache_scores - maximum[..., None])
    new_exp = jnp.exp(new_scores - maximum[..., None])
    denominator = cache_exp.sum(-1) + new_exp.sum(-1) + jnp.exp(sinks - maximum)
    cache_weights = (cache_exp / denominator[..., None]).astype(jnp.bfloat16)
    new_weights = (new_exp / denominator[..., None]).astype(jnp.bfloat16)
    attended = jnp.einsum('jbgst,jbtd->sbjgd', cache_weights.astype(jnp.float32), cache_values.astype(jnp.float32))
    attended = attended + jnp.einsum('jbgsu,ubjd->sbjgd', new_weights.astype(jnp.float32), values_new.astype(jnp.float32))
    return attended.astype(jnp.bfloat16).reshape(step_count, row_count, kv_count * group * head_dim)

def reference(hidden, joined_weight, output_weight, key_cache, value_cache, sink_logits, lengths, query_left, query_right, output_left, output_right, fitness, query_master, query_moment, output_master, output_moment):
    flat_weight = joined_weight.reshape(D, -1)

    def per_member(member_data):
        member_hidden, member_keys, member_values, member_lengths, left_q, right_q, left_o, right_o = member_data
        token_rows = member_hidden.reshape(STEPS * ROWS, D)
        projected = jnp.dot(token_rows, flat_weight, preferred_element_type=jnp.float32)
        projected = projected.reshape(STEPS * ROWS, KV_HEADS, GROUP + 2, HEAD_DIM)
        low_rank = jnp.dot(token_rows.astype(jnp.float32), left_q.T, precision=lax.Precision.HIGHEST)
        perturbed = jnp.dot(low_rank, right_q, precision=lax.Precision.HIGHEST) * (noise_scale / math.sqrt(D))
        query_part = projected[:, :, :GROUP] + perturbed.reshape(STEPS * ROWS, KV_HEADS, GROUP, HEAD_DIM)
        projected = jnp.concatenate([query_part, projected[:, :, GROUP:]], axis=2)
        projected = projected.reshape(STEPS, ROWS, KV_HEADS, GROUP + 2, HEAD_DIM)
        attended = attend(projected, member_lengths, member_keys, member_values, sink_logits)
        flat_attn = attended.reshape(STEPS * ROWS, QDIM)
        base_term = jnp.dot(flat_attn, output_weight, preferred_element_type=jnp.float32)
        low_out = jnp.dot(flat_attn.astype(jnp.float32), left_o.T, precision=lax.Precision.HIGHEST)
        extra_term = jnp.dot(low_out, right_o, precision=lax.Precision.HIGHEST) * (noise_scale / math.sqrt(QDIM))
        return (base_term + extra_term).astype(jnp.bfloat16).reshape(STEPS, ROWS, D)
    layer_output = lax.map(per_member, (hidden, key_cache, value_cache, lengths, query_left, query_right, output_left, output_right))
    weighted_query = query_right * fitness[:, None, None]
    weighted_output = output_left * fitness[:, None, None]
    query_step = jnp.einsum('mkd,mkc->dc', query_left, weighted_query, precision=lax.Precision.HIGHEST) / MEMBERS
    output_step = jnp.einsum('mkd,mkc->dc', output_right, weighted_output, precision=lax.Precision.HIGHEST) / MEMBERS
    query_momenta = moment_decay * query_moment + query_step
    output_momenta = moment_decay * output_moment + output_step
    query_weights = query_master + learn_rate * query_momenta
    output_weights = output_master + learn_rate * output_momenta
    return (layer_output, query_weights, query_momenta, output_weights, output_momenta)
```

```python
import math

import jax
import jax.numpy as jnp
from jax import lax
from jax.experimental import pallas as pl
from jax.experimental.pallas import tpu as pltpu
from jax.sharding import PartitionSpec as P

D = 2880
HEAD_DIM = 64
QDIM = 4096
LANES = 128

rotary_base = 150000.0
noise_scale = 0.5
moment_decay = 0.9
learn_rate = 0.2
masked_score = -1e30


RELAYOUT_PARTS = 8


def relayout_kernel(key_hbm, value_hbm, key_out, value_out, held, made, scratch, in_sems, out_sems):
    rows, width = key_hbm.shape
    part = width // RELAYOUT_PARTS
    tiles = part // LANES
    arrays = ((key_hbm, key_out), (value_hbm, value_out))

    def copy_in(a, i):
        at = pl.ds(i * part, part)
        return pltpu.make_async_copy(
            arrays[a][0].at[:, at], held.at[a, :, at], in_sems.at[a * RELAYOUT_PARTS + i]
        )

    def copy_out(a, i):
        at = pl.ds(i * tiles, tiles)
        return pltpu.make_async_copy(
            made.at[a, :, at, :], arrays[a][1].at[:, at, :], out_sems.at[a * RELAYOUT_PARTS + i]
        )

    steps = [(a, i) for a in range(2) for i in range(RELAYOUT_PARTS)]
    for a, i in steps:
        copy_in(a, i).start()
    for a, i in steps:
        copy_in(a, i).wait()
        for t in range(tiles):
            at = i * part + t * LANES
            scratch[a, t * rows : (t + 1) * rows, :] = held[a, :, at : at + LANES].astype(
                jnp.float32
            )
        for b in range(rows):
            made[a, b, i * tiles : (i + 1) * tiles, :] = scratch[
                a, pl.ds(b, tiles, stride=rows), :
            ].astype(jnp.bfloat16)
        copy_out(a, i).start()
    for a, i in steps:
        copy_out(a, i).wait()


def relayout(keys, values):
    rows, width = keys.shape
    out = jax.ShapeDtypeStruct((rows, width // LANES, LANES), keys.dtype)
    hbm = pl.BlockSpec(memory_space=pltpu.HBM)
    return pl.pallas_call(
        relayout_kernel,
        in_specs=[hbm] * 2,
        out_specs=[hbm] * 2,
        out_shape=[out, out],
        scratch_shapes=[
            pltpu.VMEM((2, rows, width), keys.dtype),
            pltpu.VMEM((2, rows, width // LANES, LANES), keys.dtype),
            pltpu.VMEM((2, rows * width // LANES // RELAYOUT_PARTS, LANES), jnp.float32),
            pltpu.SemaphoreType.DMA((2 * RELAYOUT_PARTS,)),
            pltpu.SemaphoreType.DMA((2 * RELAYOUT_PARTS,)),
        ],
        compiler_params=pltpu.CompilerParams(vmem_limit_bytes=60 * 1024 * 1024),
    )(keys, values)


def pack_kernel(fitness_ref, query_left, output_right, query_right, output_left, out_ref):
    score = fitness_ref[0]
    columns = query_right.shape[1]
    right = jnp.concatenate([query_right[...], output_left[...]], axis=0) * score
    left = jnp.concatenate([query_left[...], output_right[...]], axis=0)
    out_ref[:, :columns] = right.astype(jnp.bfloat16)
    pad = jnp.zeros((left.shape[0], out_ref.shape[1] - columns - left.shape[1]), jnp.float32)
    out_ref[:, columns:] = jnp.concatenate([left, pad], axis=1).astype(jnp.bfloat16)


def pack(fitness, query_left, output_right, query_right, output_left):
    rank, width = query_left.shape
    columns = query_right.shape[1]
    vmem = pl.BlockSpec(memory_space=pltpu.VMEM)
    return pl.pallas_call(
        pack_kernel,
        in_specs=[pl.BlockSpec(memory_space=pltpu.SMEM)] + [vmem] * 4,
        out_specs=vmem,
        out_shape=jax.ShapeDtypeStruct(
            (2 * rank, columns + pl.cdiv(width, LANES) * LANES), jnp.bfloat16
        ),
    )(fitness, query_left, output_right, query_right, output_left)


def update_kernel(
    start_ref,
    first_ref,
    second_ref,
    query_moment,
    query_master,
    output_moment,
    output_master,
    query_weights,
    query_momenta,
    output_weights,
    output_momenta,
    *,
    rank,
    member_count,
):
    share, columns = query_moment.shape
    start = start_ref[0]
    aligned = pl.multiple_of((start >> 7) << 7, LANES)
    shift = (2 * LANES - (start - aligned)) & (2 * LANES - 1)
    terms = []
    for ref in (first_ref, second_ref):
        left = ref[:, pl.ds(aligned, 2 * LANES)].astype(jnp.float32)
        left = pltpu.roll(left, shift, 1)[:, :LANES]
        row = lax.broadcasted_iota(jnp.int32, left.shape, 0)
        of_query = (row & (2 * rank - 1)) < rank
        for kind, chosen in enumerate((of_query, jnp.logical_not(of_query))):
            terms.append(
                lax.dot_general(
                    jnp.where(chosen, left, 0.0).astype(jnp.bfloat16),
                    ref[:, :columns],
                    (((0,), (0,)), ((), ())),
                    preferred_element_type=jnp.float32,
                )
            )
    for kind, (moment, master, weights, momenta) in enumerate(
        (
            (query_moment, query_master, query_weights, query_momenta),
            (output_moment, output_master, output_weights, output_momenta),
        )
    ):
        step = (terms[kind] + terms[2 + kind])[:share] / member_count
        new = moment_decay * moment[...] + step
        momenta[...] = new
        weights[...] = master[...] + learn_rate * new


def update(start, first, second, rank, member_count, *states):
    vmem = pl.BlockSpec(memory_space=pltpu.VMEM)

    def kernel(*refs):
        update_kernel(*refs, rank=rank, member_count=member_count)

    return pl.pallas_call(
        kernel,
        in_specs=[pl.BlockSpec(memory_space=pltpu.SMEM)] + [vmem] * 6,
        out_specs=[vmem] * 4,
        out_shape=[jax.ShapeDtypeStruct(states[0].shape, jnp.float32)] * 4,
        compiler_params=pltpu.CompilerParams(vmem_limit_bytes=16 * 1024 * 1024),
    )(start, first, second, *states)


def left_rows(left):
    hi = left.astype(jnp.bfloat16).astype(jnp.float32)
    lo = left - hi
    zeros = jnp.zeros((LANES - 24, left.shape[1]), jnp.float32)
    return jnp.concatenate([hi, hi, hi, lo, lo, lo, zeros], axis=0).astype(jnp.bfloat16)


def right_rows(right, scale):
    scaled = right * scale
    hi = scaled.astype(jnp.bfloat16).astype(jnp.float32)
    lo = scaled - hi
    zeros = jnp.zeros((LANES - 12, right.shape[1]), jnp.float32)
    return jnp.concatenate([hi, hi, lo, zeros], axis=0).astype(jnp.bfloat16)


def low_rank_operand(low):
    low = low + pltpu.roll(low, LANES - 12, 1)
    lane = lax.broadcasted_iota(jnp.int32, low.shape, 1)
    hi = low.astype(jnp.bfloat16).astype(jnp.float32)
    lo = low - hi
    return jnp.where((lane >= 4) & (lane < 8), lo, hi).astype(jnp.bfloat16)


CONTRACT_LAST = (((1,), (1,)), ((), ()))
TOGETHER = 4


def layer_kernel(lengths_ref, sink_ref, place_ref, *refs, chunk_count, own_steps):
    chunks = refs[:chunk_count]
    (
        weight_hbm,
        out_weight_hbm,
        key_hbm,
        value_hbm,
        left_q_ref,
        right_q_ref,
        left_o_ref,
        right_o_ref,
        cos_ref,
        sin_ref,
    ) = refs[chunk_count : chunk_count + 10]
    outs = refs[chunk_count + 10 : 2 * chunk_count + 10]
    (
        token_ref,
        weight_ref,
        out_weight_ref,
        key_ref,
        value_ref,
        proj_ref,
        att_ref,
        right_ref,
        sems,
        chunk_sems,
    ) = refs[2 * chunk_count + 10 :]
    chunk_rows, width = chunks[0].shape
    chunk_copies = [
        pltpu.make_async_copy(
            chunks[c], token_ref.at[pl.ds(c * chunk_rows, chunk_rows)], chunk_sems.at[c]
        )
        for c in range(chunk_count)
    ]
    weight_copy = pltpu.make_async_copy(weight_hbm, weight_ref, sems.at[0])
    key_copy = pltpu.make_async_copy(key_hbm, key_ref, sems.at[1])
    value_copy = pltpu.make_async_copy(value_hbm, value_ref, sems.at[2])
    out_weight_copy = pltpu.make_async_copy(out_weight_hbm, out_weight_ref, sems.at[3])
    for copy in chunk_copies + [weight_copy]:
        copy.start()

    seqs = key_ref.shape[0]
    total_rows = token_ref.shape[0]
    steps = total_rows // seqs
    qdim = right_q_ref.shape[1]
    group = qdim // HEAD_DIM
    tiles = qdim // LANES
    pairs = key_ref.shape[1]
    rows = group * steps

    right_ref[...] = right_rows(right_o_ref[...], noise_scale / math.sqrt(QDIM))
    left_q = left_rows(left_q_ref[...])
    for copy in chunk_copies:
        copy.wait()
    tokens = token_ref[...]
    low = lax.dot_general(
        tokens, left_q, CONTRACT_LAST, preferred_element_type=jnp.float32
    )
    low = low_rank_operand(low)
    right_q = right_rows(right_q_ref[...], noise_scale / math.sqrt(D))
    weight_copy.wait()
    for copy in (key_copy, value_copy, out_weight_copy):
        copy.start()

    cosines = cos_ref[...]
    sines = sin_ref[...]
    wide_lane = lax.broadcasted_iota(jnp.int32, cosines.shape, 1)
    first_half = (wide_lane & (HEAD_DIM - 1)) < HEAD_DIM // 2

    def rotated(t):
        swapped = jnp.where(
            first_half,
            pltpu.roll(t, LANES - HEAD_DIM // 2, 1),
            pltpu.roll(t, HEAD_DIM // 2, 1),
        )
        return t * cosines + swapped * sines

    proj = jnp.dot(tokens, weight_ref[...], preferred_element_type=jnp.float32)
    extra = jnp.dot(low, right_q, preferred_element_type=jnp.float32)
    for j in range(tiles):
        part = slice(j * LANES, (j + 1) * LANES)
        proj_ref[j] = rotated(proj[:, part] + extra[:, part]) * (HEAD_DIM**-0.5)
    tail = proj[:, qdim:]
    proj_ref[tiles] = jnp.where(wide_lane < HEAD_DIM, rotated(tail), tail)

    ring = steps // own_steps
    half_steps = own_steps // 2
    place = place_ref[0]

    def step_of(dim):
        total = jnp.zeros((steps, steps), jnp.int32)
        row = lax.broadcasted_iota(jnp.int32, (steps, steps), dim)
        at = 0
        for k in range(2):
            for order in range(ring):
                distance = (order + 1) // 2
                chunk = (place + ring + (distance if order % 2 else -distance)) & (ring - 1)
                first = chunk * own_steps + k * half_steps
                total = jnp.where(row >= at, first + row - at, total)
                at += half_steps
        return total

    bias = jnp.where(step_of(1) <= step_of(0), 0.0, masked_score)
    bias = jnp.concatenate([bias] * group, axis=0)
    sinks = jnp.concatenate(
        [jnp.full((steps, 1), sink_ref[g], jnp.float32) for g in range(group)], axis=0
    )
    pair = lax.broadcasted_iota(jnp.int32, (1, pairs), 1)
    low_lanes = lax.broadcasted_iota(jnp.int32, (steps, LANES), 1) < HEAD_DIM

    def several(i, carry):
        members = [i * TOGETHER + u for u in range(TOGETHER)]
        evens, odds, news, scored = [], [], [], []
        for b in members:
            even, odd = [], []
            for j in range(tiles):
                t = proj_ref[j, pl.ds(b, steps, stride=seqs), :]
                r = pltpu.roll(t, HEAD_DIM, 1)
                even += [jnp.where(low_lanes, t, 0.0), jnp.where(low_lanes, r, 0.0)]
                odd += [jnp.where(low_lanes, 0.0, r), jnp.where(low_lanes, 0.0, t)]
            evens.append(jnp.concatenate(even, axis=0).astype(jnp.bfloat16))
            odds.append(jnp.concatenate(odd, axis=0).astype(jnp.bfloat16))
            news.append(proj_ref[tiles, pl.ds(b, steps, stride=seqs), :].astype(jnp.bfloat16))
        for u, b in enumerate(members):
            length = lengths_ref[b]
            keys = key_ref[b]

            def scores(query, parity):
                valid = jnp.where(2 * pair + parity < length, 0.0, masked_score)
                return (
                    lax.dot_general(
                        query, keys, CONTRACT_LAST, preferred_element_type=jnp.float32
                    )
                    + valid
                )

            s_new = (
                lax.dot_general(
                    evens[u], news[u], CONTRACT_LAST, preferred_element_type=jnp.float32
                )
                + bias
            )
            scored.append((scores(evens[u], 0), scores(odds[u], 1), s_new))
        for u, b in enumerate(members):
            s_even, s_odd, s_new = scored[u]
            values = value_ref[b]
            top = jnp.maximum(
                jnp.max(jnp.maximum(s_even, s_odd), axis=1, keepdims=True),
                jnp.maximum(jnp.max(s_new, axis=1, keepdims=True), sinks),
            )
            p_even = jnp.exp(s_even - top)
            p_odd = jnp.exp(s_odd - top)
            p_new = jnp.exp(s_new - top)
            total = (
                jnp.sum(p_even + p_odd, axis=1, keepdims=True)
                + jnp.sum(p_new, axis=1, keepdims=True)
                + jnp.exp(sinks - top)
            )
            a_even = jnp.dot(
                p_even.astype(jnp.bfloat16), values, preferred_element_type=jnp.float32
            )
            a_odd = jnp.dot(
                p_odd.astype(jnp.bfloat16), values, preferred_element_type=jnp.float32
            ) + jnp.dot(p_new.astype(jnp.bfloat16), news[u], preferred_element_type=jnp.float32)
            inverse = 1.0 / total
            a_even = a_even * inverse
            a_odd = a_odd * inverse
            for j in range(tiles):
                g = 2 * j
                e0 = a_even[g * steps : (g + 1) * steps]
                o0 = a_odd[g * steps : (g + 1) * steps]
                e1 = a_even[(g + 1) * steps : (g + 2) * steps]
                o1 = a_odd[(g + 1) * steps : (g + 2) * steps]
                tile = jnp.where(
                    low_lanes, e0 + pltpu.roll(o0, HEAD_DIM, 1), o1 + pltpu.roll(e1, HEAD_DIM, 1)
                )
                att_ref[j, pl.ds(b, steps, stride=seqs), :] = tile
        return carry

    key_copy.wait()
    value_copy.wait()
    lax.fori_loop(0, seqs // TOGETHER, several, 0)

    out_weight_copy.wait()
    attended = jnp.concatenate([att_ref[j] for j in range(tiles)], axis=1).astype(jnp.bfloat16)
    low = lax.dot_general(
        attended, left_rows(left_o_ref[...]), CONTRACT_LAST, preferred_element_type=jnp.float32
    )
    low = low_rank_operand(low)
    for at in range(0, width, 768):
        to = min(at + 768, width)
        share = lax.dot_general(
            attended, out_weight_ref[at:to, :], CONTRACT_LAST, preferred_element_type=jnp.float32
        ) + jnp.dot(low, right_ref[:, at:to], preferred_element_type=jnp.float32)
        share = share.astype(jnp.bfloat16)
        for c in range(chunk_count):
            outs[c][:, at:to] = share[c * chunk_rows : (c + 1) * chunk_rows]


def layer(lengths, sinks, place, chunks, weight, out_weight, keys, values, own_steps, *operands):
    chunk_rows, width = chunks[0].shape
    rows = chunk_rows * len(chunks)
    joined = weight.shape[1]
    qdim = operands[1].shape[1]
    vmem = pl.BlockSpec(memory_space=pltpu.VMEM)
    smem = pl.BlockSpec(memory_space=pltpu.SMEM)
    hbm = pl.BlockSpec(memory_space=pltpu.HBM)
    either = pl.BlockSpec(memory_space=pl.ANY)

    def kernel(*refs):
        layer_kernel(*refs, chunk_count=len(chunks), own_steps=own_steps)

    return pl.pallas_call(
        kernel,
        in_specs=[smem] * 3 + [either] * len(chunks) + [hbm] * 4 + [vmem] * len(operands),
        out_specs=[vmem] * len(chunks),
        out_shape=[jax.ShapeDtypeStruct((chunk_rows, width), jnp.bfloat16)] * len(chunks),
        scratch_shapes=[
            pltpu.VMEM((rows, width), jnp.bfloat16),
            pltpu.VMEM(weight.shape, jnp.bfloat16),
            pltpu.VMEM(out_weight.shape, jnp.bfloat16),
            pltpu.VMEM(keys.shape, jnp.bfloat16),
            pltpu.VMEM(values.shape, jnp.bfloat16),
            pltpu.VMEM((joined // LANES, rows, LANES), jnp.float32),
            pltpu.VMEM((qdim // LANES, rows, LANES), jnp.float32),
            pltpu.VMEM((LANES, width), jnp.bfloat16),
            pltpu.SemaphoreType.DMA((4,)),
            pltpu.SemaphoreType.DMA((len(chunks),)),
        ],
        compiler_params=pltpu.CompilerParams(vmem_limit_bytes=57 * 1024 * 1024),
    )(lengths, sinks, place, *chunks, weight, out_weight, keys, values, *operands)


def shards(
    hidden,
    joined_weight,
    output_weight,
    key_cache,
    value_cache,
    sink_logits,
    lengths,
    query_left,
    query_right,
    output_left,
    output_right,
    fitness,
    query_master,
    query_moment,
    output_master,
    output_moment,
):
    ring = lax.axis_size("head")
    place = lax.axis_index("head")
    right_pairs = [(i, (i + 1) % ring) for i in range(ring)]
    left_pairs = [(i, (i - 1) % ring) for i in range(ring)]

    def to_right(x):
        return lax.ppermute(x, "head", right_pairs)

    def to_left(x):
        return lax.ppermute(x, "head", left_pairs)

    _, own_steps, row_count, width = hidden.shape
    half_steps = own_steps // 2
    flat_weight = joined_weight[:, 0, :]

    member_count = lax.axis_size("member")
    factors = pack(fitness, query_left[0], output_right[0], query_right[0], output_left[0])
    distance = member_count // 2
    while distance > 0:
        other = lax.ppermute(
            factors, "member", [(i, i ^ distance) for i in range(member_count)]
        )
        if distance > 1:
            factors = jnp.concatenate([factors, other], axis=0)
        distance //= 2

    own = [
        hidden[0, k * half_steps : (k + 1) * half_steps].reshape(-1, width) for k in range(2)
    ]
    chunks = []
    for k in range(2):
        from_left, from_right = [own[k]], [own[k]]
        for _ in range(ring // 2 - 1):
            from_left.append(to_right(from_left[-1]))
            from_right.append(to_left(from_right[-1]))
        far = to_right(from_left[-1]) if k == 0 else to_left(from_right[-1])
        chunks.append(own[k])
        for distance in range(1, ring // 2):
            chunks += [from_right[distance], from_left[distance]]
        chunks.append(far)

    keys, values = relayout(key_cache[0, 0], value_cache[0, 0])

    offsets = [0]
    for distance in range(1, ring // 2):
        offsets += [distance, -distance]
    offsets.append(ring // 2)
    chunk_ids = jnp.mod(place + jnp.array(offsets, jnp.int32), ring)
    halves = jnp.arange(2, dtype=jnp.int32)[:, None, None] * half_steps
    steps = (
        chunk_ids[None, :, None] * own_steps
        + halves
        + jnp.arange(half_steps, dtype=jnp.int32)[None, None, :]
    ).reshape(-1)
    half_dim = HEAD_DIM // 2
    lane_ids = jnp.arange(LANES, dtype=jnp.int32)
    exponents = (lane_ids % half_dim).astype(jnp.float32) * (-2.0 / HEAD_DIM)
    frequency = jnp.power(jnp.float32(rotary_base), exponents)
    positions = steps[:, None] + lengths[0][None, :]
    angles = positions.astype(jnp.float32)[..., None] * frequency
    sign = jnp.where(lane_ids % HEAD_DIM < half_dim, -1.0, 1.0).astype(jnp.float32)
    cosines = jnp.cos(angles).reshape(-1, LANES)
    sines = (jnp.sin(angles) * sign).reshape(-1, LANES)

    shares = layer(
        lengths[0],
        sink_logits,
        place.reshape(1).astype(jnp.int32),
        chunks,
        flat_weight,
        output_weight.T,
        keys,
        values,
        own_steps,
        query_left[0],
        query_right[0],
        output_left[0],
        output_right[0],
        cosines,
        sines,
    )

    row_share = query_master.shape[0]
    start = query_right.shape[2] + lax.axis_index("member") * row_share
    updated = update(
        start.reshape(1).astype(jnp.int32),
        factors,
        other,
        query_right.shape[1],
        member_count,
        query_moment,
        query_master,
        output_moment,
        output_master,
    )

    results = []
    for k in range(2):
        at = {offset: shares[k * ring + i] for i, offset in enumerate(offsets)}

        def plus(received, offset):
            return (received.astype(jnp.float32) + at[offset].astype(jnp.float32)).astype(
                jnp.bfloat16
            )

        last = ring // 2 - 1
        if k == 0:
            rightward = plus(to_right(at[last + 1]), last)
            leftward = at[-last]
        else:
            rightward = at[last]
            leftward = plus(to_left(at[last + 1]), -last)
        for distance in range(last - 1, 0, -1):
            rightward = plus(to_right(rightward), distance)
            leftward = plus(to_left(leftward), -distance)
        results.append((to_right(rightward), to_left(leftward), at[0]))
    mine, updated = lax.optimization_barrier(([r[2] for r in results], tuple(updated)))
    layer_output = []
    for (from_left, from_right, _), own_share in zip(results, mine):
        total = (
            from_left.astype(jnp.float32)
            + from_right.astype(jnp.float32)
            + own_share.astype(jnp.float32)
        )
        layer_output.append(total.astype(jnp.bfloat16).reshape(half_steps, row_count, width))
    layer_output = jnp.concatenate(layer_output, axis=0)[None]
    return (layer_output,) + updated


def solution(mesh):
    placed = (
        P("member", "head", None, None),
        P(None, "head", None),
        P("head", None),
        P("member", "head", None, None),
        P("member", "head", None, None),
        P("head"),
        P("member", None),
        P("member", None, None),
        P("member", None, "head"),
        P("member", None, "head"),
        P("member", None, None),
        P("member"),
        P("member", "head"),
        P("member", "head"),
        P("member", "head"),
        P("member", "head"),
    )
    return jax.shard_map(
        shards,
        mesh=mesh,
        in_specs=placed,
        out_specs=(
            P("member", "head", None, None),
            P("member", "head"),
            P("member", "head"),
            P("member", "head"),
            P("member", "head"),
        ),
        check_vma=False,
    )
```

```python
import functools
import math

import jax
import jax.numpy as jnp
from jax import lax
from jax.experimental import pallas as pl
from jax.experimental.pallas import tpu as pltpu
from jax.sharding import PartitionSpec as P

D = 2880
HEAD_DIM = 64
QDIM = 4096
LANES = 128

rotary_base = 150000.0
noise_scale = 0.5
moment_decay = 0.9
learn_rate = 0.2
masked_score = -1e30


RELAYOUT_PARTS = 8


def relayout_kernel(key_hbm, value_hbm, key_out, value_out, held, made, scratch, in_sems, out_sems):
    rows, width = key_hbm.shape
    part = width // RELAYOUT_PARTS
    tiles = part // LANES
    arrays = ((key_hbm, key_out), (value_hbm, value_out))

    def copy_in(a, i):
        at = pl.ds(i * part, part)
        return pltpu.make_async_copy(
            arrays[a][0].at[:, at], held.at[a, :, at], in_sems.at[a * RELAYOUT_PARTS + i]
        )

    def copy_out(a, i):
        at = pl.ds(i * tiles, tiles)
        return pltpu.make_async_copy(
            made.at[a, :, at, :], arrays[a][1].at[:, at, :], out_sems.at[a * RELAYOUT_PARTS + i]
        )

    steps = [(a, i) for a in range(2) for i in range(RELAYOUT_PARTS)]
    for a, i in steps:
        copy_in(a, i).start()
    for a, i in steps:
        copy_in(a, i).wait()
        for t in range(tiles):
            at = i * part + t * LANES
            scratch[a, t * rows : (t + 1) * rows, :] = held[a, :, at : at + LANES].astype(
                jnp.float32
            )
        for b in range(rows):
            made[a, b, i * tiles : (i + 1) * tiles, :] = scratch[
                a, pl.ds(b, tiles, stride=rows), :
            ].astype(jnp.bfloat16)
        copy_out(a, i).start()
    for a, i in steps:
        copy_out(a, i).wait()


def relayout(keys, values):
    rows, width = keys.shape
    out = jax.ShapeDtypeStruct((rows, width // LANES, LANES), keys.dtype)
    hbm = pl.BlockSpec(memory_space=pltpu.HBM)
    return pl.pallas_call(
        relayout_kernel,
        in_specs=[hbm] * 2,
        out_specs=[hbm] * 2,
        out_shape=[out, out],
        scratch_shapes=[
            pltpu.VMEM((2, rows, width), keys.dtype),
            pltpu.VMEM((2, rows, width // LANES, LANES), keys.dtype),
            pltpu.VMEM((2, rows * width // LANES // RELAYOUT_PARTS, LANES), jnp.float32),
            pltpu.SemaphoreType.DMA((2 * RELAYOUT_PARTS,)),
            pltpu.SemaphoreType.DMA((2 * RELAYOUT_PARTS,)),
        ],
        compiler_params=pltpu.CompilerParams(vmem_limit_bytes=60 * 1024 * 1024),
    )(keys, values)


def pack_kernel(fitness_ref, query_left, output_right, query_right, output_left, out_ref):
    score = fitness_ref[0]
    columns = query_right.shape[1]
    right = jnp.concatenate([query_right[...], output_left[...]], axis=0) * score
    left = jnp.concatenate([query_left[...], output_right[...]], axis=0)
    out_ref[:, :columns] = right.astype(jnp.bfloat16)
    pad = jnp.zeros((left.shape[0], out_ref.shape[1] - columns - left.shape[1]), jnp.float32)
    out_ref[:, columns:] = jnp.concatenate([left, pad], axis=1).astype(jnp.bfloat16)


def pack(fitness, query_left, output_right, query_right, output_left):
    rank, width = query_left.shape
    columns = query_right.shape[1]
    vmem = pl.BlockSpec(memory_space=pltpu.VMEM)
    return pl.pallas_call(
        pack_kernel,
        in_specs=[pl.BlockSpec(memory_space=pltpu.SMEM)] + [vmem] * 4,
        out_specs=vmem,
        out_shape=jax.ShapeDtypeStruct(
            (2 * rank, columns + pl.cdiv(width, LANES) * LANES), jnp.bfloat16
        ),
    )(fitness, query_left, output_right, query_right, output_left)


def update_kernel(
    start_ref,
    first_ref,
    second_ref,
    query_moment,
    query_master,
    output_moment,
    output_master,
    query_weights,
    query_momenta,
    output_weights,
    output_momenta,
    *,
    rank,
    member_count,
):
    share, columns = query_moment.shape
    start = start_ref[0]
    aligned = pl.multiple_of((start >> 7) << 7, LANES)
    shift = (2 * LANES - (start - aligned)) & (2 * LANES - 1)
    terms = []
    for ref in (first_ref, second_ref):
        left = ref[:, pl.ds(aligned, 2 * LANES)].astype(jnp.float32)
        left = pltpu.roll(left, shift, 1)[:, :LANES]
        row = lax.broadcasted_iota(jnp.int32, left.shape, 0)
        of_query = (row & (2 * rank - 1)) < rank
        for kind, chosen in enumerate((of_query, jnp.logical_not(of_query))):
            terms.append(
                lax.dot_general(
                    jnp.where(chosen, left, 0.0).astype(jnp.bfloat16),
                    ref[:, :columns],
                    (((0,), (0,)), ((), ())),
                    preferred_element_type=jnp.float32,
                )
            )
    for kind, (moment, master, weights, momenta) in enumerate(
        (
            (query_moment, query_master, query_weights, query_momenta),
            (output_moment, output_master, output_weights, output_momenta),
        )
    ):
        step = (terms[kind] + terms[2 + kind])[:share] / member_count
        new = moment_decay * moment[...] + step
        momenta[...] = new
        weights[...] = master[...] + learn_rate * new


def update(start, first, second, rank, member_count, *states):
    vmem = pl.BlockSpec(memory_space=pltpu.VMEM)

    def kernel(*refs):
        update_kernel(*refs, rank=rank, member_count=member_count)

    return pl.pallas_call(
        kernel,
        in_specs=[pl.BlockSpec(memory_space=pltpu.SMEM)] + [vmem] * 6,
        out_specs=[vmem] * 4,
        out_shape=[jax.ShapeDtypeStruct(states[0].shape, jnp.float32)] * 4,
        compiler_params=pltpu.CompilerParams(vmem_limit_bytes=16 * 1024 * 1024),
    )(start, first, second, *states)


def left_rows(left):
    hi = left.astype(jnp.bfloat16).astype(jnp.float32)
    lo = left - hi
    zeros = jnp.zeros((LANES - 24, left.shape[1]), jnp.float32)
    return jnp.concatenate([hi, hi, hi, lo, lo, lo, zeros], axis=0).astype(jnp.bfloat16)


def right_rows(right, scale):
    scaled = right * scale
    hi = scaled.astype(jnp.bfloat16).astype(jnp.float32)
    lo = scaled - hi
    zeros = jnp.zeros((LANES - 12, right.shape[1]), jnp.float32)
    return jnp.concatenate([hi, hi, lo, zeros], axis=0).astype(jnp.bfloat16)


def low_rank_operand(low):
    low = low + pltpu.roll(low, LANES - 12, 1)
    lane = lax.broadcasted_iota(jnp.int32, low.shape, 1)
    hi = low.astype(jnp.bfloat16).astype(jnp.float32)
    lo = low - hi
    return jnp.where((lane >= 4) & (lane < 8), lo, hi).astype(jnp.bfloat16)


CONTRACT_LAST = (((1,), (1,)), ((), ()))


def project(tokens, weight_wait, weight_ref, left_q, right_q, cosines, sines, store):
    qdim = right_q.shape[1]
    tiles = qdim // LANES
    low = lax.dot_general(
        tokens, left_rows(left_q), CONTRACT_LAST, preferred_element_type=jnp.float32
    )
    low = low_rank_operand(low)
    right = right_rows(right_q, noise_scale / math.sqrt(D))
    extra = jnp.dot(low, right, preferred_element_type=jnp.float32)
    lane = lax.broadcasted_iota(jnp.int32, cosines.shape, 1)
    first_half = (lane & (HEAD_DIM - 1)) < HEAD_DIM // 2

    def rotated(t):
        swapped = jnp.where(
            first_half,
            pltpu.roll(t, LANES - HEAD_DIM // 2, 1),
            pltpu.roll(t, HEAD_DIM // 2, 1),
        )
        return t * cosines + swapped * sines

    weight_wait()
    proj = jnp.dot(tokens, weight_ref[...], preferred_element_type=jnp.float32)
    for j in range(tiles):
        part = slice(j * LANES, (j + 1) * LANES)
        store(j, rotated(proj[:, part] + extra[:, part]) * (HEAD_DIM**-0.5))
    tail = proj[:, qdim:]
    store(tiles, jnp.where(lane < HEAD_DIM, rotated(tail), tail))


def project_kernel(*refs, chunk_count, first_row):
    chunks = refs[:chunk_count]
    weight_hbm, left_q_ref, right_q_ref, cos_ref, sin_ref, out_ref = refs[
        chunk_count : chunk_count + 6
    ]
    token_ref, weight_ref, sems = refs[chunk_count + 6 :]
    chunk_rows = chunks[0].shape[0]
    rows = chunk_rows * chunk_count
    copies = [
        pltpu.make_async_copy(
            chunks[c], token_ref.at[pl.ds(c * chunk_rows, chunk_rows)], sems.at[c]
        )
        for c in range(chunk_count)
    ]
    weight_copy = pltpu.make_async_copy(weight_hbm, weight_ref, sems.at[chunk_count])
    for copy in copies + [weight_copy]:
        copy.start()
    for copy in copies:
        copy.wait()
    here = pl.ds(first_row, rows)

    def store(j, value):
        out_ref[j] = value

    project(
        token_ref[...],
        weight_copy.wait,
        weight_ref,
        left_q_ref[...],
        right_q_ref[...],
        cos_ref[here, :],
        sin_ref[here, :],
        store,
    )


def project_chunks(chunks, first_row, weight, left_q, right_q, cosines, sines):
    chunk_rows, width = chunks[0].shape
    rows = chunk_rows * len(chunks)
    vmem = pl.BlockSpec(memory_space=pltpu.VMEM)
    either = pl.BlockSpec(memory_space=pl.ANY)

    def kernel(*refs):
        project_kernel(*refs, chunk_count=len(chunks), first_row=first_row)

    return pl.pallas_call(
        kernel,
        in_specs=[either] * (len(chunks) + 1) + [vmem] * 4,
        out_specs=vmem,
        out_shape=jax.ShapeDtypeStruct((weight.shape[1] // LANES, rows, LANES), jnp.float32),
        scratch_shapes=[
            pltpu.VMEM((rows, width), jnp.bfloat16),
            pltpu.VMEM(weight.shape, jnp.bfloat16),
            pltpu.SemaphoreType.DMA((len(chunks) + 1,)),
        ],
        compiler_params=pltpu.CompilerParams(vmem_limit_bytes=57 * 1024 * 1024),
    )(*chunks, weight, left_q, right_q, cosines, sines)


TOGETHER = 2


def layer_kernel(lengths_ref, sink_ref, place_ref, *refs, chunk_count, ready_count, own_steps):
    chunks = refs[:chunk_count]
    ready = refs[chunk_count : chunk_count + ready_count]
    refs = refs[chunk_count + ready_count :]
    (
        weight_hbm,
        out_weight_hbm,
        key_hbm,
        value_hbm,
        left_q_ref,
        right_q_ref,
        left_o_ref,
        right_o_ref,
        cos_ref,
        sin_ref,
    ) = refs[:10]
    (
        token_ref,
        weight_ref,
        out_weight_ref,
        key_ref,
        value_ref,
        proj_ref,
        att_ref,
        right_ref,
        bias_ref,
        sems,
        chunk_sems,
    ) = refs[-11:]
    outs = refs[10:-11]
    chunk_rows, width = chunks[0].shape
    copies = [
        pltpu.make_async_copy(
            chunks[c], token_ref.at[pl.ds(c * chunk_rows, chunk_rows)], chunk_sems.at[c]
        )
        for c in range(chunk_count)
    ]
    weight_copy = pltpu.make_async_copy(weight_hbm, weight_ref, sems.at[0])
    key_copy = pltpu.make_async_copy(key_hbm, key_ref, sems.at[1])
    value_copy = pltpu.make_async_copy(value_hbm, value_ref, sems.at[2])
    out_weight_copy = pltpu.make_async_copy(out_weight_hbm, out_weight_ref, sems.at[3])
    ready_copies = []
    first_row = 0
    for i in range(ready_count):
        count = ready[i].shape[1]
        ready_copies.append(
            pltpu.make_async_copy(
                ready[i], proj_ref.at[:, pl.ds(first_row, count), :], chunk_sems.at[chunk_count + i]
            )
        )
        first_row += count
    for copy in copies + [weight_copy] + ready_copies + [key_copy, value_copy, out_weight_copy]:
        copy.start()

    seqs = key_ref.shape[0]
    total_rows = proj_ref.shape[1]
    steps = total_rows // seqs
    qdim = right_q_ref.shape[1]
    group = qdim // HEAD_DIM
    tiles = qdim // LANES
    pairs = key_ref.shape[1]
    rows = group * steps

    right_ref[...] = right_rows(right_o_ref[...], noise_scale / math.sqrt(QDIM))
    for copy in copies:
        copy.wait()
    here = pl.ds(first_row, chunk_count * chunk_rows)

    def store(j, value):
        proj_ref[j, here, :] = value

    project(
        token_ref[...],
        weight_copy.wait,
        weight_ref,
        left_q_ref[...],
        right_q_ref[...],
        cos_ref[here, :],
        sin_ref[here, :],
        store,
    )

    ring = steps // own_steps
    place = place_ref[0]

    def step_of(dim):
        total = jnp.zeros((steps, steps), jnp.int32)
        row = lax.broadcasted_iota(jnp.int32, (steps, steps), dim)
        for order in range(ring):
            distance = (order + 1) // 2
            chunk = (place + ring + (distance if order % 2 else -distance)) & (ring - 1)
            at = order * own_steps
            total = jnp.where(row >= at, chunk * own_steps + row - at, total)
        return total

    bias = jnp.where(step_of(1) <= step_of(0), 0.0, masked_score)
    column = lax.broadcasted_iota(jnp.int32, (steps, LANES - steps), 1)
    for g in range(group):
        bias_ref[g * steps : (g + 1) * steps, :] = jnp.concatenate(
            [bias, jnp.where(column == 0, sink_ref[g], masked_score)], axis=1
        )
    pair = lax.broadcasted_iota(jnp.int32, (1, pairs), 1)
    low_lanes = lax.broadcasted_iota(jnp.int32, (steps, LANES), 1) < HEAD_DIM

    def several(i, carry):
        members = [i * TOGETHER + u for u in range(TOGETHER)]
        evens, odds, news, scored = [], [], [], []
        for b in members:
            even, odd = [], []
            for j in range(tiles):
                t = proj_ref[j, pl.ds(b, steps, stride=seqs), :]
                r = pltpu.roll(t, HEAD_DIM, 1)
                even += [jnp.where(low_lanes, t, 0.0), jnp.where(low_lanes, r, 0.0)]
                odd += [jnp.where(low_lanes, 0.0, r), jnp.where(low_lanes, 0.0, t)]
            evens.append(jnp.concatenate(even, axis=0).astype(jnp.bfloat16))
            odds.append(jnp.concatenate(odd, axis=0).astype(jnp.bfloat16))
            new_pair = proj_ref[tiles, pl.ds(b, steps, stride=seqs), :]
            nothing = jnp.zeros((LANES - steps, LANES), jnp.float32)
            news.append(jnp.concatenate([new_pair, nothing], axis=0).astype(jnp.bfloat16))
        for u, b in enumerate(members):
            length = lengths_ref[b]
            keys = key_ref[b]

            def scores(query, parity):
                valid = jnp.where(2 * pair + parity < length, 0.0, masked_score)
                return (
                    lax.dot_general(
                        query, keys, CONTRACT_LAST, preferred_element_type=jnp.float32
                    )
                    + valid
                )

            s_new = (
                lax.dot_general(
                    evens[u], news[u], CONTRACT_LAST, preferred_element_type=jnp.float32
                )
                + bias_ref[...]
            )
            scored.append((scores(evens[u], 0), scores(odds[u], 1), s_new))
        for u, b in enumerate(members):
            s_even, s_odd, s_new = scored[u]
            values = value_ref[b]

            def folded(join, even, odd, new):
                return functools.reduce(
                    join,
                    [x[:, i : i + LANES] for x in (even, odd) for i in range(0, pairs, LANES)],
                    new,
                )

            top = jnp.max(folded(jnp.maximum, s_even, s_odd, s_new), axis=1, keepdims=True)
            p_even = jnp.exp(s_even - top)
            p_odd = jnp.exp(s_odd - top)
            p_new = jnp.exp(s_new - top)
            total = jnp.sum(folded(jnp.add, p_even, p_odd, p_new), axis=1, keepdims=True)
            a_even = jnp.dot(
                p_even.astype(jnp.bfloat16), values, preferred_element_type=jnp.float32
            )
            a_odd = jnp.dot(
                p_odd.astype(jnp.bfloat16), values, preferred_element_type=jnp.float32
            ) + jnp.dot(p_new.astype(jnp.bfloat16), news[u], preferred_element_type=jnp.float32)
            inverse = 1.0 / total
            a_even = a_even * inverse
            a_odd = a_odd * inverse
            for j in range(tiles):
                g = 2 * j
                e0 = a_even[g * steps : (g + 1) * steps]
                o0 = a_odd[g * steps : (g + 1) * steps]
                e1 = a_even[(g + 1) * steps : (g + 2) * steps]
                o1 = a_odd[(g + 1) * steps : (g + 2) * steps]
                tile = jnp.where(
                    low_lanes, e0 + pltpu.roll(o0, HEAD_DIM, 1), o1 + pltpu.roll(e1, HEAD_DIM, 1)
                )
                att_ref[j, pl.ds(b, steps, stride=seqs), :] = tile
        return carry

    for copy in ready_copies + [key_copy, value_copy]:
        copy.wait()
    lax.fori_loop(0, seqs // TOGETHER, several, 0)

    out_weight_copy.wait()
    attended = jnp.concatenate([att_ref[j] for j in range(tiles)], axis=1).astype(jnp.bfloat16)
    low = lax.dot_general(
        attended, left_rows(left_o_ref[...]), CONTRACT_LAST, preferred_element_type=jnp.float32
    )
    low = low_rank_operand(low)
    for at in range(0, width, 768):
        to = min(at + 768, width)
        share = lax.dot_general(
            attended, out_weight_ref[at:to, :], CONTRACT_LAST, preferred_element_type=jnp.float32
        ) + jnp.dot(low, right_ref[:, at:to], preferred_element_type=jnp.float32)
        share = share.astype(jnp.bfloat16)
        part = total_rows // len(outs)
        for c, out in enumerate(outs):
            out[:, at:to] = share[c * part : (c + 1) * part]


def layer(
    lengths, sinks, place, chunks, ready, out_parts, weight, out_weight, keys, values, own_steps, *operands
):
    chunk_rows, width = chunks[0].shape
    rows = sum(r.shape[1] for r in ready) + chunk_rows * len(chunks)
    joined = weight.shape[1]
    qdim = operands[1].shape[1]
    group_rows = rows // values.shape[0] * qdim // HEAD_DIM
    vmem = pl.BlockSpec(memory_space=pltpu.VMEM)
    smem = pl.BlockSpec(memory_space=pltpu.SMEM)
    either = pl.BlockSpec(memory_space=pl.ANY)

    def kernel(*refs):
        layer_kernel(
            *refs, chunk_count=len(chunks), ready_count=len(ready), own_steps=own_steps
        )

    return pl.pallas_call(
        kernel,
        in_specs=[smem] * 3 + [either] * (len(chunks) + len(ready) + 4) + [vmem] * len(operands),
        out_specs=[vmem] * out_parts,
        out_shape=[jax.ShapeDtypeStruct((rows // out_parts, width), jnp.bfloat16)] * out_parts,
        scratch_shapes=[
            pltpu.VMEM((chunk_rows * len(chunks), width), jnp.bfloat16),
            pltpu.VMEM(weight.shape, jnp.bfloat16),
            pltpu.VMEM(out_weight.shape, jnp.bfloat16),
            pltpu.VMEM(keys.shape, jnp.bfloat16),
            pltpu.VMEM(values.shape, jnp.bfloat16),
            pltpu.VMEM((joined // LANES, rows, LANES), jnp.float32),
            pltpu.VMEM((qdim // LANES, rows, LANES), jnp.float32),
            pltpu.VMEM((LANES, width), jnp.bfloat16),
            pltpu.VMEM((group_rows, LANES), jnp.float32),
            pltpu.SemaphoreType.DMA((4,)),
            pltpu.SemaphoreType.DMA((len(chunks) + len(ready),)),
        ],
        compiler_params=pltpu.CompilerParams(vmem_limit_bytes=57 * 1024 * 1024),
    )(lengths, sinks, place, *chunks, *ready, weight, out_weight, keys, values, *operands)


def shards(
    hidden,
    joined_weight,
    output_weight,
    key_cache,
    value_cache,
    sink_logits,
    lengths,
    query_left,
    query_right,
    output_left,
    output_right,
    fitness,
    query_master,
    query_moment,
    output_master,
    output_moment,
):
    ring = lax.axis_size("head")
    place = lax.axis_index("head")
    right_pairs = [(i, (i + 1) % ring) for i in range(ring)]
    left_pairs = [(i, (i - 1) % ring) for i in range(ring)]

    def to_right(x):
        return lax.ppermute(x, "head", right_pairs)

    def to_left(x):
        return lax.ppermute(x, "head", left_pairs)

    _, own_steps, row_count, width = hidden.shape
    flat_weight = joined_weight[:, 0, :]

    member_count = lax.axis_size("member")
    factors = pack(fitness, query_left[0], output_right[0], query_right[0], output_left[0])
    held = [factors, factors]

    def exchange(distance, after):
        if distance < 1:
            return after
        mine = held[0]
        if held[1] is not held[0]:
            mine = jnp.concatenate(held, axis=0)
        mine, after = lax.optimization_barrier((mine, after))
        pairs = [(i, i ^ distance) for i in range(member_count)]
        held[0], held[1] = mine, lax.ppermute(mine, "member", pairs)
        return after

    keys, values = relayout(key_cache[0, 0], value_cache[0, 0])

    offsets = [0]
    for distance in range(1, ring // 2):
        offsets += [distance, -distance]
    offsets.append(ring // 2)
    chunk_ids = jnp.mod(place + jnp.array(offsets, jnp.int32), ring)
    steps = (
        chunk_ids[:, None] * own_steps + jnp.arange(own_steps, dtype=jnp.int32)[None, :]
    ).reshape(-1)
    half_dim = HEAD_DIM // 2
    lane_ids = jnp.arange(LANES, dtype=jnp.int32)
    exponents = (lane_ids % half_dim).astype(jnp.float32) * (-2.0 / HEAD_DIM)
    frequency = jnp.power(jnp.float32(rotary_base), exponents)
    positions = steps[:, None] + lengths[0][None, :]
    angles = positions.astype(jnp.float32)[..., None] * frequency
    sign = jnp.where(lane_ids % HEAD_DIM < half_dim, -1.0, 1.0).astype(jnp.float32)
    cosines = jnp.cos(angles).reshape(-1, LANES)
    sines = (jnp.sin(angles) * sign).reshape(-1, LANES)

    own = hidden[0].reshape(-1, width)
    half = own.shape[0] // 2
    exchange(member_count // 2, ())
    from_left, from_right = [own, to_right(own)], [own, to_left(own)]
    keys, values, cosines, sines, onward, back = lax.optimization_barrier(
        (keys, values, cosines, sines, from_left[1], from_right[1])
    )
    from_left.append(to_right(onward))
    from_right.append(to_left(back))
    exchange(member_count // 4, from_left[1])
    own_rows = own.shape[0]
    factor_operands = (flat_weight, query_left[0], query_right[0], cosines, sines)
    for distance in range(3, ring // 2):
        from_left.append(to_right(from_left[-1]))
        from_right.append(to_left(from_right[-1]))
    near = [own]
    for distance in range(1, ring // 2):
        near += [from_right[distance], from_left[distance]]
    early = ring - 3
    exchange(member_count // 8, from_left[-2])
    first_projected = project_chunks(near[:early], 0, *factor_operands)
    first_projected, onward, back = lax.optimization_barrier(
        (first_projected, from_left[-1][:half], from_right[-1][half:])
    )
    far = [to_right(onward), to_left(back)]
    second_projected = project_chunks(near[early:], early * own_rows, *factor_operands)
    exchange(member_count // 16, from_left[-1])
    projected = [first_projected, second_projected]
    shares = layer(
        lengths[0],
        sink_logits,
        place.reshape(1).astype(jnp.int32),
        far,
        projected,
        2 * ring,
        flat_weight,
        output_weight.T,
        keys,
        values,
        own_steps,
        query_left[0],
        query_right[0],
        output_left[0],
        output_right[0],
        cosines,
        sines,
    )

    exchange(member_count // 32, shares[0])
    row_share = query_master.shape[0]
    start = query_right.shape[2] + lax.axis_index("member") * row_share
    updated = update(
        start.reshape(1).astype(jnp.int32),
        *held,
        query_right.shape[1],
        member_count,
        query_moment,
        query_master,
        output_moment,
        output_master,
    )

    results = []
    for k in range(2):
        at = {offset: shares[2 * i + k] for i, offset in enumerate(offsets)}

        def plus(received, offset):
            return (received.astype(jnp.float32) + at[offset].astype(jnp.float32)).astype(
                jnp.bfloat16
            )

        last = ring // 2 - 1
        if k == 0:
            rightward = plus(to_right(at[last + 1]), last)
            leftward = at[-last]
        else:
            rightward = at[last]
            leftward = plus(to_left(at[last + 1]), -last)
        for distance in range(last - 1, 0, -1):
            rightward = plus(to_right(rightward), distance)
            leftward = plus(to_left(leftward), -distance)
        results.append((to_right(rightward), to_left(leftward), at[0]))
    mine, updated = lax.optimization_barrier(([r[2] for r in results], tuple(updated)))
    layer_output = []
    for (from_left, from_right, _), own_share in zip(results, mine):
        total = (
            from_left.astype(jnp.float32)
            + from_right.astype(jnp.float32)
            + own_share.astype(jnp.float32)
        )
        layer_output.append(total.astype(jnp.bfloat16).reshape(own_steps // 2, row_count, width))
    layer_output = jnp.concatenate(layer_output, axis=0)[None]
    return (layer_output,) + updated


def solution(mesh):
    placed = (
        P("member", "head", None, None),
        P(None, "head", None),
        P("head", None),
        P("member", "head", None, None),
        P("member", "head", None, None),
        P("head"),
        P("member", None),
        P("member", None, None),
        P("member", None, "head"),
        P("member", None, "head"),
        P("member", None, None),
        P("member"),
        P("member", "head"),
        P("member", "head"),
        P("member", "head"),
        P("member", "head"),
    )
    return jax.shard_map(
        shards,
        mesh=mesh,
        in_specs=placed,
        out_specs=(
            P("member", "head", None, None),
            P("member", "head"),
            P("member", "head"),
            P("member", "head"),
            P("member", "head"),
        ),
        check_vma=False,
    )
```

```python
import functools
import math

import jax
import jax.numpy as jnp
from jax import lax
from jax.experimental import pallas as pl
from jax.experimental.pallas import tpu as pltpu
from jax.sharding import PartitionSpec as P

D = 2880
HEAD_DIM = 64
QDIM = 4096
LANES = 128

rotary_base = 150000.0
noise_scale = 0.5
moment_decay = 0.9
learn_rate = 0.2
masked_score = -1e30


RELAYOUT_PARTS = 8


def relayout_kernel(key_hbm, value_hbm, key_out, value_out, held, made, scratch, in_sems, out_sems):
    rows, width = key_hbm.shape
    part = width // RELAYOUT_PARTS
    tiles = part // LANES
    arrays = ((key_hbm, key_out), (value_hbm, value_out))

    def copy_in(a, i):
        at = pl.ds(i * part, part)
        return pltpu.make_async_copy(
            arrays[a][0].at[:, at], held.at[a, :, at], in_sems.at[a * RELAYOUT_PARTS + i]
        )

    def copy_out(a, i):
        at = pl.ds(i * tiles, tiles)
        return pltpu.make_async_copy(
            made.at[a, :, at, :], arrays[a][1].at[:, at, :], out_sems.at[a * RELAYOUT_PARTS + i]
        )

    steps = [(a, i) for a in range(2) for i in range(RELAYOUT_PARTS)]
    for a, i in steps:
        copy_in(a, i).start()
    for a, i in steps:
        copy_in(a, i).wait()
        for t in range(tiles):
            at = i * part + t * LANES
            scratch[a, t * rows : (t + 1) * rows, :] = held[a, :, at : at + LANES].astype(
                jnp.float32
            )
        for b in range(rows):
            made[a, b, i * tiles : (i + 1) * tiles, :] = scratch[
                a, pl.ds(b, tiles, stride=rows), :
            ].astype(jnp.bfloat16)
        copy_out(a, i).start()
    for a, i in steps:
        copy_out(a, i).wait()


def relayout(keys, values):
    rows, width = keys.shape
    out = jax.ShapeDtypeStruct((rows, width // LANES, LANES), keys.dtype)
    hbm = pl.BlockSpec(memory_space=pltpu.HBM)
    return pl.pallas_call(
        relayout_kernel,
        in_specs=[hbm] * 2,
        out_specs=[hbm] * 2,
        out_shape=[out, out],
        scratch_shapes=[
            pltpu.VMEM((2, rows, width), keys.dtype),
            pltpu.VMEM((2, rows, width // LANES, LANES), keys.dtype),
            pltpu.VMEM((2, rows * width // LANES // RELAYOUT_PARTS, LANES), jnp.float32),
            pltpu.SemaphoreType.DMA((2 * RELAYOUT_PARTS,)),
            pltpu.SemaphoreType.DMA((2 * RELAYOUT_PARTS,)),
        ],
        compiler_params=pltpu.CompilerParams(vmem_limit_bytes=60 * 1024 * 1024),
    )(keys, values)


def pack_kernel(fitness_ref, query_left, output_right, query_right, output_left, out_ref):
    score = fitness_ref[0]
    columns = query_right.shape[1]
    right = jnp.concatenate([query_right[...], output_left[...]], axis=0) * score
    left = jnp.concatenate([query_left[...], output_right[...]], axis=0)
    out_ref[:, :columns] = right.astype(jnp.bfloat16)
    pad = jnp.zeros((left.shape[0], out_ref.shape[1] - columns - left.shape[1]), jnp.float32)
    out_ref[:, columns:] = jnp.concatenate([left, pad], axis=1).astype(jnp.bfloat16)


def pack(fitness, query_left, output_right, query_right, output_left):
    rank, width = query_left.shape
    columns = query_right.shape[1]
    vmem = pl.BlockSpec(memory_space=pltpu.VMEM)
    return pl.pallas_call(
        pack_kernel,
        in_specs=[pl.BlockSpec(memory_space=pltpu.SMEM)] + [vmem] * 4,
        out_specs=vmem,
        out_shape=jax.ShapeDtypeStruct(
            (2 * rank, columns + pl.cdiv(width, LANES) * LANES), jnp.bfloat16
        ),
    )(fitness, query_left, output_right, query_right, output_left)


def update_kernel(
    start_ref,
    first_ref,
    second_ref,
    query_moment,
    query_master,
    output_moment,
    output_master,
    query_weights,
    query_momenta,
    output_weights,
    output_momenta,
    *,
    rank,
    member_count,
):
    share, columns = query_moment.shape
    start = start_ref[0]
    aligned = pl.multiple_of((start >> 7) << 7, LANES)
    shift = (2 * LANES - (start - aligned)) & (2 * LANES - 1)
    terms = []
    for ref in (first_ref, second_ref):
        left = ref[:, pl.ds(aligned, 2 * LANES)].astype(jnp.float32)
        left = pltpu.roll(left, shift, 1)[:, :LANES]
        row = lax.broadcasted_iota(jnp.int32, left.shape, 0)
        of_query = (row & (2 * rank - 1)) < rank
        for kind, chosen in enumerate((of_query, jnp.logical_not(of_query))):
            terms.append(
                lax.dot_general(
                    jnp.where(chosen, left, 0.0).astype(jnp.bfloat16),
                    ref[:, :columns],
                    (((0,), (0,)), ((), ())),
                    preferred_element_type=jnp.float32,
                )
            )
    for kind, (moment, master, weights, momenta) in enumerate(
        (
            (query_moment, query_master, query_weights, query_momenta),
            (output_moment, output_master, output_weights, output_momenta),
        )
    ):
        step = (terms[kind] + terms[2 + kind])[:share] / member_count
        new = moment_decay * moment[...] + step
        momenta[...] = new
        weights[...] = master[...] + learn_rate * new


def update(start, first, second, rank, member_count, *states):
    vmem = pl.BlockSpec(memory_space=pltpu.VMEM)

    def kernel(*refs):
        update_kernel(*refs, rank=rank, member_count=member_count)

    return pl.pallas_call(
        kernel,
        in_specs=[pl.BlockSpec(memory_space=pltpu.SMEM)] + [vmem] * 6,
        out_specs=[vmem] * 4,
        out_shape=[jax.ShapeDtypeStruct(states[0].shape, jnp.float32)] * 4,
        compiler_params=pltpu.CompilerParams(vmem_limit_bytes=16 * 1024 * 1024),
    )(start, first, second, *states)


def left_rows(left):
    hi = left.astype(jnp.bfloat16).astype(jnp.float32)
    lo = left - hi
    zeros = jnp.zeros((LANES - 24, left.shape[1]), jnp.float32)
    return jnp.concatenate([hi, hi, hi, lo, lo, lo, zeros], axis=0).astype(jnp.bfloat16)


def right_rows(right, scale):
    scaled = right * scale
    hi = scaled.astype(jnp.bfloat16).astype(jnp.float32)
    lo = scaled - hi
    zeros = jnp.zeros((LANES - 12, right.shape[1]), jnp.float32)
    return jnp.concatenate([hi, hi, lo, zeros], axis=0).astype(jnp.bfloat16)


def low_rank_operand(low):
    low = low + pltpu.roll(low, LANES - 12, 1)
    lane = lax.broadcasted_iota(jnp.int32, low.shape, 1)
    hi = low.astype(jnp.bfloat16).astype(jnp.float32)
    lo = low - hi
    return jnp.where((lane >= 4) & (lane < 8), lo, hi).astype(jnp.bfloat16)


CONTRACT_LAST = (((1,), (1,)), ((), ()))


def project(tokens, weight_ref, left_q, right_q, cosines, sines, store):
    qdim = right_q.shape[1]
    tiles = qdim // LANES
    low = lax.dot_general(
        tokens, left_rows(left_q), CONTRACT_LAST, preferred_element_type=jnp.float32
    )
    low = low_rank_operand(low)
    right = right_rows(right_q, noise_scale / math.sqrt(D))
    extra = jnp.dot(low, right, preferred_element_type=jnp.float32)
    lane = lax.broadcasted_iota(jnp.int32, cosines.shape, 1)
    first_half = (lane & (HEAD_DIM - 1)) < HEAD_DIM // 2

    def rotated(t):
        swapped = jnp.where(
            first_half,
            pltpu.roll(t, LANES - HEAD_DIM // 2, 1),
            pltpu.roll(t, HEAD_DIM // 2, 1),
        )
        return t * cosines + swapped * sines

    proj = jnp.dot(tokens, weight_ref[...], preferred_element_type=jnp.float32)
    for j in range(tiles):
        part = slice(j * LANES, (j + 1) * LANES)
        store(j, rotated(proj[:, part] + extra[:, part]) * (HEAD_DIM**-0.5))
    tail = proj[:, qdim:]
    store(tiles, jnp.where(lane < HEAD_DIM, rotated(tail), tail))


def project_kernel(*refs, chunk_count, first_row):
    chunks = refs[:chunk_count]
    weight_ref, left_q_ref, right_q_ref, cos_ref, sin_ref, out_ref = refs[
        chunk_count : chunk_count + 6
    ]
    token_ref, sems = refs[chunk_count + 6 :]
    chunk_rows = chunks[0].shape[0]
    rows = chunk_rows * chunk_count
    copies = [
        pltpu.make_async_copy(
            chunks[c], token_ref.at[pl.ds(c * chunk_rows, chunk_rows)], sems.at[c]
        )
        for c in range(chunk_count)
    ]
    for copy in copies:
        copy.start()
    for copy in copies:
        copy.wait()
    here = pl.ds(first_row, rows)

    def store(j, value):
        out_ref[j] = value

    project(
        token_ref[...],
        weight_ref,
        left_q_ref[...],
        right_q_ref[...],
        cos_ref[here, :],
        sin_ref[here, :],
        store,
    )


def project_chunks(chunks, first_row, weight, left_q, right_q, cosines, sines):
    chunk_rows, width = chunks[0].shape
    rows = chunk_rows * len(chunks)
    vmem = pl.BlockSpec(memory_space=pltpu.VMEM)
    either = pl.BlockSpec(memory_space=pl.ANY)

    def kernel(*refs):
        project_kernel(*refs, chunk_count=len(chunks), first_row=first_row)

    return pl.pallas_call(
        kernel,
        in_specs=[either] * len(chunks) + [vmem] * 5,
        out_specs=vmem,
        out_shape=jax.ShapeDtypeStruct((weight.shape[1] // LANES, rows, LANES), jnp.float32),
        scratch_shapes=[
            pltpu.VMEM((rows, width), jnp.bfloat16),
            pltpu.SemaphoreType.DMA((len(chunks),)),
        ],
        compiler_params=pltpu.CompilerParams(vmem_limit_bytes=38 * 1024 * 1024),
    )(*chunks, weight, left_q, right_q, cosines, sines)


TOGETHER = 4


def layer_kernel(lengths_ref, sink_ref, place_ref, *refs, chunk_count, ready_count, own_steps):
    chunks = refs[:chunk_count]
    ready = refs[chunk_count : chunk_count + ready_count]
    refs = refs[chunk_count + ready_count :]
    (
        out_weight_hbm,
        key_hbm,
        value_hbm,
        weight_ref,
        left_q_ref,
        right_q_ref,
        left_o_ref,
        right_o_ref,
        cos_ref,
        sin_ref,
    ) = refs[:10]
    (
        token_ref,
        out_weight_ref,
        key_ref,
        value_ref,
        proj_ref,
        att_ref,
        right_ref,
        bias_ref,
        sems,
        chunk_sems,
    ) = refs[-10:]
    outs = refs[10:-10]
    chunk_rows, width = chunks[0].shape
    copies = [
        pltpu.make_async_copy(
            chunks[c], token_ref.at[pl.ds(c * chunk_rows, chunk_rows)], chunk_sems.at[c]
        )
        for c in range(chunk_count)
    ]
    key_copy = pltpu.make_async_copy(key_hbm, key_ref, sems.at[0])
    value_copy = pltpu.make_async_copy(value_hbm, value_ref, sems.at[1])
    out_weight_copy = pltpu.make_async_copy(out_weight_hbm, out_weight_ref, sems.at[2])
    ready_copies = []
    first_row = 0
    for i in range(ready_count):
        count = ready[i].shape[1]
        ready_copies.append(
            pltpu.make_async_copy(
                ready[i], proj_ref.at[:, pl.ds(first_row, count), :], chunk_sems.at[chunk_count + i]
            )
        )
        first_row += count
    for copy in copies + ready_copies + [key_copy, value_copy, out_weight_copy]:
        copy.start()

    seqs = key_ref.shape[0]
    total_rows = proj_ref.shape[1]
    steps = total_rows // seqs
    qdim = right_q_ref.shape[1]
    group = qdim // HEAD_DIM
    tiles = qdim // LANES
    pairs = key_ref.shape[1]
    rows = group * steps

    right_ref[...] = right_rows(right_o_ref[...], noise_scale / math.sqrt(QDIM))
    for copy in copies:
        copy.wait()
    here = pl.ds(first_row, chunk_count * chunk_rows)

    def store(j, value):
        proj_ref[j, here, :] = value

    project(
        token_ref[...],
        weight_ref,
        left_q_ref[...],
        right_q_ref[...],
        cos_ref[here, :],
        sin_ref[here, :],
        store,
    )

    ring = steps // own_steps
    place = place_ref[0]

    def step_of(dim):
        total = jnp.zeros((steps, steps), jnp.int32)
        row = lax.broadcasted_iota(jnp.int32, (steps, steps), dim)
        for order in range(ring):
            distance = (order + 1) // 2
            chunk = (place + ring + (distance if order % 2 else -distance)) & (ring - 1)
            at = order * own_steps
            total = jnp.where(row >= at, chunk * own_steps + row - at, total)
        return total

    bias = jnp.where(step_of(1) <= step_of(0), 0.0, masked_score)
    column = lax.broadcasted_iota(jnp.int32, (steps, LANES - steps), 1)
    for g in range(group):
        bias_ref[g * steps : (g + 1) * steps, :] = jnp.concatenate(
            [bias, jnp.where(column == 0, sink_ref[g], masked_score)], axis=1
        )
    pair = lax.broadcasted_iota(jnp.int32, (1, pairs), 1)
    low_lanes = lax.broadcasted_iota(jnp.int32, (steps, LANES), 1) < HEAD_DIM

    def several(i, carry):
        members = [i * TOGETHER + u for u in range(TOGETHER)]
        evens, odds, news, scored = [], [], [], []
        for b in members:
            even, odd = [], []
            for j in range(tiles):
                t = proj_ref[j, pl.ds(b, steps, stride=seqs), :]
                r = pltpu.roll(t, HEAD_DIM, 1)
                even += [jnp.where(low_lanes, t, 0.0), jnp.where(low_lanes, r, 0.0)]
                odd += [jnp.where(low_lanes, 0.0, r), jnp.where(low_lanes, 0.0, t)]
            evens.append(jnp.concatenate(even, axis=0).astype(jnp.bfloat16))
            odds.append(jnp.concatenate(odd, axis=0).astype(jnp.bfloat16))
            new_pair = proj_ref[tiles, pl.ds(b, steps, stride=seqs), :]
            nothing = jnp.zeros((LANES - steps, LANES), jnp.float32)
            news.append(jnp.concatenate([new_pair, nothing], axis=0).astype(jnp.bfloat16))
        for u, b in enumerate(members):
            length = lengths_ref[b]
            keys = key_ref[b]

            def scores(query, parity):
                valid = jnp.where(2 * pair + parity < length, 0.0, masked_score)
                return (
                    lax.dot_general(
                        query, keys, CONTRACT_LAST, preferred_element_type=jnp.float32
                    )
                    + valid
                )

            s_new = (
                lax.dot_general(
                    evens[u], news[u], CONTRACT_LAST, preferred_element_type=jnp.float32
                )
                + bias_ref[...]
            )
            scored.append((scores(evens[u], 0), scores(odds[u], 1), s_new))
        for u, b in enumerate(members):
            s_even, s_odd, s_new = scored[u]
            values = value_ref[b]

            def folded(join, even, odd, new):
                return functools.reduce(
                    join,
                    [x[:, i : i + LANES] for x in (even, odd) for i in range(0, pairs, LANES)],
                    new,
                )

            top = jnp.max(folded(jnp.maximum, s_even, s_odd, s_new), axis=1, keepdims=True)
            p_even = jnp.exp(s_even - top)
            p_odd = jnp.exp(s_odd - top)
            p_new = jnp.exp(s_new - top)
            total = jnp.sum(folded(jnp.add, p_even, p_odd, p_new), axis=1, keepdims=True)
            a_even = jnp.dot(
                p_even.astype(jnp.bfloat16), values, preferred_element_type=jnp.float32
            )
            a_odd = jnp.dot(
                p_odd.astype(jnp.bfloat16), values, preferred_element_type=jnp.float32
            ) + jnp.dot(p_new.astype(jnp.bfloat16), news[u], preferred_element_type=jnp.float32)
            inverse = 1.0 / total
            a_even = a_even * inverse
            a_odd = a_odd * inverse
            for j in range(tiles):
                g = 2 * j
                e0 = a_even[g * steps : (g + 1) * steps]
                o0 = a_odd[g * steps : (g + 1) * steps]
                e1 = a_even[(g + 1) * steps : (g + 2) * steps]
                o1 = a_odd[(g + 1) * steps : (g + 2) * steps]
                tile = jnp.where(
                    low_lanes, e0 + pltpu.roll(o0, HEAD_DIM, 1), o1 + pltpu.roll(e1, HEAD_DIM, 1)
                )
                att_ref[j, pl.ds(b, steps, stride=seqs), :] = tile
        return carry

    for copy in ready_copies + [key_copy, value_copy]:
        copy.wait()
    lax.fori_loop(0, seqs // TOGETHER, several, 0)

    out_weight_copy.wait()
    attended = jnp.concatenate([att_ref[j] for j in range(tiles)], axis=1).astype(jnp.bfloat16)
    low = lax.dot_general(
        attended, left_rows(left_o_ref[...]), CONTRACT_LAST, preferred_element_type=jnp.float32
    )
    low = low_rank_operand(low)
    for at in range(0, width, 768):
        to = min(at + 768, width)
        share = lax.dot_general(
            attended, out_weight_ref[at:to, :], CONTRACT_LAST, preferred_element_type=jnp.float32
        ) + jnp.dot(low, right_ref[:, at:to], preferred_element_type=jnp.float32)
        share = share.astype(jnp.bfloat16)
        part = total_rows // len(outs)
        for c, out in enumerate(outs):
            out[:, at:to] = share[c * part : (c + 1) * part]


def layer(
    lengths, sinks, place, chunks, ready, out_parts, weight, out_weight, keys, values, own_steps, *operands
):
    chunk_rows, width = chunks[0].shape
    rows = sum(r.shape[1] for r in ready) + chunk_rows * len(chunks)
    joined = weight.shape[1]
    qdim = operands[1].shape[1]
    group_rows = rows // values.shape[0] * qdim // HEAD_DIM
    vmem = pl.BlockSpec(memory_space=pltpu.VMEM)
    smem = pl.BlockSpec(memory_space=pltpu.SMEM)
    either = pl.BlockSpec(memory_space=pl.ANY)

    def kernel(*refs):
        layer_kernel(
            *refs, chunk_count=len(chunks), ready_count=len(ready), own_steps=own_steps
        )

    return pl.pallas_call(
        kernel,
        in_specs=[smem] * 3 + [either] * (len(chunks) + len(ready) + 3) + [vmem] * (1 + len(operands)),
        out_specs=[vmem] * out_parts,
        out_shape=[jax.ShapeDtypeStruct((rows // out_parts, width), jnp.bfloat16)] * out_parts,
        scratch_shapes=[
            pltpu.VMEM((chunk_rows * len(chunks), width), jnp.bfloat16),
            pltpu.VMEM(out_weight.shape, jnp.bfloat16),
            pltpu.VMEM(keys.shape, jnp.bfloat16),
            pltpu.VMEM(values.shape, jnp.bfloat16),
            pltpu.VMEM((joined // LANES, rows, LANES), jnp.float32),
            pltpu.VMEM((qdim // LANES, rows, LANES), jnp.float32),
            pltpu.VMEM((LANES, width), jnp.bfloat16),
            pltpu.VMEM((group_rows, LANES), jnp.float32),
            pltpu.SemaphoreType.DMA((3,)),
            pltpu.SemaphoreType.DMA((len(chunks) + len(ready),)),
        ],
        compiler_params=pltpu.CompilerParams(vmem_limit_bytes=38 * 1024 * 1024),
    )(lengths, sinks, place, *chunks, *ready, out_weight, keys, values, weight, *operands)


def shards(
    hidden,
    joined_weight,
    output_weight,
    key_cache,
    value_cache,
    sink_logits,
    lengths,
    query_left,
    query_right,
    output_left,
    output_right,
    fitness,
    query_master,
    query_moment,
    output_master,
    output_moment,
):
    ring = lax.axis_size("head")
    place = lax.axis_index("head")
    right_pairs = [(i, (i + 1) % ring) for i in range(ring)]
    left_pairs = [(i, (i - 1) % ring) for i in range(ring)]

    def to_right(x):
        return lax.ppermute(x, "head", right_pairs)

    def to_left(x):
        return lax.ppermute(x, "head", left_pairs)

    _, own_steps, row_count, width = hidden.shape
    flat_weight = joined_weight[:, 0, :]

    member_count = lax.axis_size("member")
    factors = pack(fitness, query_left[0], output_right[0], query_right[0], output_left[0])
    held = [factors, factors]

    def exchange(distance, after):
        if distance < 1:
            return after
        mine = held[0]
        if held[1] is not held[0]:
            mine = jnp.concatenate(held, axis=0)
        mine, after = lax.optimization_barrier((mine, after))
        pairs = [(i, i ^ distance) for i in range(member_count)]
        held[0], held[1] = mine, lax.ppermute(mine, "member", pairs)
        return after

    offsets = [0]
    for distance in range(1, ring // 2):
        offsets += [distance, -distance]
    offsets.append(ring // 2)
    chunk_ids = jnp.mod(place + jnp.array(offsets, jnp.int32), ring)
    steps = (
        chunk_ids[:, None] * own_steps + jnp.arange(own_steps, dtype=jnp.int32)[None, :]
    ).reshape(-1)
    half_dim = HEAD_DIM // 2
    lane_ids = jnp.arange(LANES, dtype=jnp.int32)
    exponents = (lane_ids % half_dim).astype(jnp.float32) * (-2.0 / HEAD_DIM)
    frequency = jnp.power(jnp.float32(rotary_base), exponents)
    positions = steps[:, None] + lengths[0][None, :]
    angles = positions.astype(jnp.float32)[..., None] * frequency
    sign = jnp.where(lane_ids % HEAD_DIM < half_dim, -1.0, 1.0).astype(jnp.float32)
    cosines = jnp.cos(angles).reshape(-1, LANES)
    sines = (jnp.sin(angles) * sign).reshape(-1, LANES)

    own = hidden[0].reshape(-1, width)
    half = own.shape[0] // 2
    exchange(member_count // 2, ())
    from_left, from_right = [own, to_right(own)], [own, to_left(own)]
    cosines, sines, onward, back = lax.optimization_barrier(
        (cosines, sines, from_left[1], from_right[1])
    )
    from_left.append(to_right(onward))
    from_right.append(to_left(back))
    exchange(member_count // 4, from_left[1])
    cached = lax.optimization_barrier((key_cache, value_cache, onward))
    keys, values = relayout(cached[0][0, 0], cached[1][0, 0])
    own_rows = own.shape[0]
    factor_operands = (flat_weight, query_left[0], query_right[0], cosines, sines)
    for distance in range(3, ring // 2):
        keys, values, onward, back = lax.optimization_barrier(
            (keys, values, from_left[-1], from_right[-1])
        )
        from_left.append(to_right(onward))
        from_right.append(to_left(back))
    near = [own]
    for distance in range(1, ring // 2):
        near += [from_right[distance], from_left[distance]]
    early = ring - 3
    exchange(member_count // 8, from_left[-2])
    first_projected = project_chunks(near[:early], 0, *factor_operands)
    first_projected, onward, back = lax.optimization_barrier(
        (first_projected, from_left[-1][:half], from_right[-1][half:])
    )
    far = [to_right(onward), to_left(back)]
    second_projected = project_chunks(near[early:], early * own_rows, *factor_operands)
    exchange(member_count // 16, from_left[-1])
    projected = [first_projected, second_projected]
    shares = layer(
        lengths[0],
        sink_logits,
        place.reshape(1).astype(jnp.int32),
        far,
        projected,
        2 * ring,
        flat_weight,
        output_weight.T,
        keys,
        values,
        own_steps,
        query_left[0],
        query_right[0],
        output_left[0],
        output_right[0],
        cosines,
        sines,
    )

    exchange(member_count // 32, shares[0])
    row_share = query_master.shape[0]
    start = query_right.shape[2] + lax.axis_index("member") * row_share
    updated = update(
        start.reshape(1).astype(jnp.int32),
        *held,
        query_right.shape[1],
        member_count,
        query_moment,
        query_master,
        output_moment,
        output_master,
    )

    at = {
        (offset, k): shares[2 * i + k] for i, offset in enumerate(offsets) for k in range(2)
    }
    last = ring // 2 - 1
    chains = [
        dict(way=to_right, sign=1, k=0, next=last, moving=at[last + 1, 0]),
        dict(way=to_left, sign=-1, k=1, next=last, moving=at[last + 1, 1]),
        dict(way=to_left, sign=-1, k=0, next=last - 1, moving=at[-last, 0]),
        dict(way=to_right, sign=1, k=1, next=last - 1, moving=at[last, 1]),
    ]
    before = None
    for chain in chains:
        chain["moving"] = chain["way"](chain["moving"])
    for _ in range(last):
        for chain in chains:
            if chain["next"] == 0:
                continue
            mine = at[chain["sign"] * chain["next"], chain["k"]]
            if before is not None:
                mine, before = lax.optimization_barrier((mine, before))
            before = (chain["moving"].astype(jnp.float32) + mine.astype(jnp.float32)).astype(
                jnp.bfloat16
            )
            chain["moving"] = chain["way"](before)
            chain["next"] -= 1
    results = [
        (chains[0]["moving"], chains[2]["moving"], at[0, 0]),
        (chains[3]["moving"], chains[1]["moving"], at[0, 1]),
    ]
    mine, updated = lax.optimization_barrier(([r[2] for r in results], tuple(updated)))
    layer_output = []
    for (from_left, from_right, _), own_share in zip(results, mine):
        total = (
            from_left.astype(jnp.float32)
            + from_right.astype(jnp.float32)
            + own_share.astype(jnp.float32)
        )
        layer_output.append(total.astype(jnp.bfloat16).reshape(own_steps // 2, row_count, width))
    layer_output = jnp.concatenate(layer_output, axis=0)[None]
    return (layer_output,) + updated


def solution(mesh):
    placed = (
        P("member", "head", None, None),
        P(None, "head", None),
        P("head", None),
        P("member", "head", None, None),
        P("member", "head", None, None),
        P("head"),
        P("member", None),
        P("member", None, None),
        P("member", None, "head"),
        P("member", None, "head"),
        P("member", None, None),
        P("member"),
        P("member", "head"),
        P("member", "head"),
        P("member", "head"),
        P("member", "head"),
    )
    return jax.shard_map(
        shards,
        mesh=mesh,
        in_specs=placed,
        out_specs=(
            P("member", "head", None, None),
            P("member", "head"),
            P("member", "head"),
            P("member", "head"),
            P("member", "head"),
        ),
        check_vma=False,
    )
```

```python
import functools
import math

import jax
import jax.numpy as jnp
from jax import lax
from jax.experimental import pallas as pl
from jax.experimental.pallas import tpu as pltpu
from jax.sharding import PartitionSpec as P

D = 2880
HEAD_DIM = 64
QDIM = 4096
LANES = 128

rotary_base = 150000.0
noise_scale = 0.5
moment_decay = 0.9
learn_rate = 0.2
masked_score = -1e30


RELAYOUT_PARTS = 8


def relayout_kernel(key_hbm, value_hbm, key_out, value_out, held, made, scratch, in_sems, out_sems):
    rows, width = key_hbm.shape
    part = width // RELAYOUT_PARTS
    tiles = part // LANES
    arrays = ((key_hbm, key_out), (value_hbm, value_out))

    def copy_in(a, i):
        at = pl.ds(i * part, part)
        return pltpu.make_async_copy(
            arrays[a][0].at[:, at], held.at[a, :, at], in_sems.at[a * RELAYOUT_PARTS + i]
        )

    def copy_out(a, i):
        at = pl.ds(i * tiles, tiles)
        return pltpu.make_async_copy(
            made.at[a, :, at, :], arrays[a][1].at[:, at, :], out_sems.at[a * RELAYOUT_PARTS + i]
        )

    steps = [(a, i) for a in range(2) for i in range(RELAYOUT_PARTS)]
    for a, i in steps:
        copy_in(a, i).start()
    for a, i in steps:
        copy_in(a, i).wait()
        for t in range(tiles):
            at = i * part + t * LANES
            scratch[a, t * rows : (t + 1) * rows, :] = held[a, :, at : at + LANES].astype(
                jnp.float32
            )
        for b in range(rows):
            made[a, b, i * tiles : (i + 1) * tiles, :] = scratch[
                a, pl.ds(b, tiles, stride=rows), :
            ].astype(jnp.bfloat16)
        copy_out(a, i).start()
    for a, i in steps:
        copy_out(a, i).wait()


def relayout(keys, values):
    rows, width = keys.shape
    out = jax.ShapeDtypeStruct((rows, width // LANES, LANES), keys.dtype)
    hbm = pl.BlockSpec(memory_space=pltpu.HBM)
    return pl.pallas_call(
        relayout_kernel,
        in_specs=[hbm] * 2,
        out_specs=[hbm] * 2,
        out_shape=[out, out],
        scratch_shapes=[
            pltpu.VMEM((2, rows, width), keys.dtype),
            pltpu.VMEM((2, rows, width // LANES, LANES), keys.dtype),
            pltpu.VMEM((2, rows * width // LANES // RELAYOUT_PARTS, LANES), jnp.float32),
            pltpu.SemaphoreType.DMA((2 * RELAYOUT_PARTS,)),
            pltpu.SemaphoreType.DMA((2 * RELAYOUT_PARTS,)),
        ],
        compiler_params=pltpu.CompilerParams(vmem_limit_bytes=60 * 1024 * 1024),
    )(keys, values)


def pack_kernel(fitness_ref, query_left, output_right, query_right, output_left, out_ref):
    score = fitness_ref[0]
    columns = query_right.shape[1]
    right = jnp.concatenate([query_right[...], output_left[...]], axis=0) * score
    left = jnp.concatenate([query_left[...], output_right[...]], axis=0)
    out_ref[:, :columns] = right.astype(jnp.bfloat16)
    pad = jnp.zeros((left.shape[0], out_ref.shape[1] - columns - left.shape[1]), jnp.float32)
    out_ref[:, columns:] = jnp.concatenate([left, pad], axis=1).astype(jnp.bfloat16)


def pack(fitness, query_left, output_right, query_right, output_left):
    rank, width = query_left.shape
    columns = query_right.shape[1]
    vmem = pl.BlockSpec(memory_space=pltpu.VMEM)
    return pl.pallas_call(
        pack_kernel,
        in_specs=[pl.BlockSpec(memory_space=pltpu.SMEM)] + [vmem] * 4,
        out_specs=vmem,
        out_shape=jax.ShapeDtypeStruct(
            (2 * rank, columns + pl.cdiv(width, LANES) * LANES), jnp.bfloat16
        ),
    )(fitness, query_left, output_right, query_right, output_left)


def update_kernel(
    start_ref,
    first_ref,
    second_ref,
    query_moment,
    query_master,
    output_moment,
    output_master,
    query_weights,
    query_momenta,
    output_weights,
    output_momenta,
    *,
    rank,
    member_count,
):
    share, columns = query_moment.shape
    start = start_ref[0]
    aligned = pl.multiple_of((start >> 7) << 7, LANES)
    shift = (2 * LANES - (start - aligned)) & (2 * LANES - 1)
    terms = []
    for ref in (first_ref, second_ref):
        left = ref[:, pl.ds(aligned, 2 * LANES)].astype(jnp.float32)
        left = pltpu.roll(left, shift, 1)[:, :LANES]
        row = lax.broadcasted_iota(jnp.int32, left.shape, 0)
        of_query = (row & (2 * rank - 1)) < rank
        for kind, chosen in enumerate((of_query, jnp.logical_not(of_query))):
            terms.append(
                lax.dot_general(
                    jnp.where(chosen, left, 0.0).astype(jnp.bfloat16),
                    ref[:, :columns],
                    (((0,), (0,)), ((), ())),
                    preferred_element_type=jnp.float32,
                )
            )
    for kind, (moment, master, weights, momenta) in enumerate(
        (
            (query_moment, query_master, query_weights, query_momenta),
            (output_moment, output_master, output_weights, output_momenta),
        )
    ):
        step = (terms[kind] + terms[2 + kind])[:share] / member_count
        new = moment_decay * moment[...] + step
        momenta[...] = new
        weights[...] = master[...] + learn_rate * new


def update(start, first, second, rank, member_count, *states):
    vmem = pl.BlockSpec(memory_space=pltpu.VMEM)

    def kernel(*refs):
        update_kernel(*refs, rank=rank, member_count=member_count)

    return pl.pallas_call(
        kernel,
        in_specs=[pl.BlockSpec(memory_space=pltpu.SMEM)] + [vmem] * 6,
        out_specs=[vmem] * 4,
        out_shape=[jax.ShapeDtypeStruct(states[0].shape, jnp.float32)] * 4,
        compiler_params=pltpu.CompilerParams(vmem_limit_bytes=16 * 1024 * 1024),
    )(start, first, second, *states)


def left_rows(left):
    hi = left.astype(jnp.bfloat16).astype(jnp.float32)
    lo = left - hi
    zeros = jnp.zeros((LANES - 24, left.shape[1]), jnp.float32)
    return jnp.concatenate([hi, hi, hi, lo, lo, lo, zeros], axis=0).astype(jnp.bfloat16)


def right_rows(right, scale):
    scaled = right * scale
    hi = scaled.astype(jnp.bfloat16).astype(jnp.float32)
    lo = scaled - hi
    zeros = jnp.zeros((LANES - 12, right.shape[1]), jnp.float32)
    return jnp.concatenate([hi, hi, lo, zeros], axis=0).astype(jnp.bfloat16)


def low_rank_operand(low):
    low = low + pltpu.roll(low, LANES - 12, 1)
    lane = lax.broadcasted_iota(jnp.int32, low.shape, 1)
    hi = low.astype(jnp.bfloat16).astype(jnp.float32)
    lo = low - hi
    return jnp.where((lane >= 4) & (lane < 8), lo, hi).astype(jnp.bfloat16)


CONTRACT_LAST = (((1,), (1,)), ((), ()))


def project(tokens, weight_ref, left_q, right_q, cosines, sines, store):
    qdim = right_q.shape[1]
    tiles = qdim // LANES
    low = lax.dot_general(
        tokens, left_rows(left_q), CONTRACT_LAST, preferred_element_type=jnp.float32
    )
    low = low_rank_operand(low)
    right = right_rows(right_q, noise_scale / math.sqrt(D))
    extra = jnp.dot(low, right, preferred_element_type=jnp.float32)
    lane = lax.broadcasted_iota(jnp.int32, cosines.shape, 1)
    first_half = (lane & (HEAD_DIM - 1)) < HEAD_DIM // 2

    def rotated(t):
        swapped = jnp.where(
            first_half,
            pltpu.roll(t, LANES - HEAD_DIM // 2, 1),
            pltpu.roll(t, HEAD_DIM // 2, 1),
        )
        return t * cosines + swapped * sines

    proj = jnp.dot(tokens, weight_ref[...], preferred_element_type=jnp.float32)
    for j in range(tiles):
        part = slice(j * LANES, (j + 1) * LANES)
        store(j, rotated(proj[:, part] + extra[:, part]) * (HEAD_DIM**-0.5))
    tail = proj[:, qdim:]
    store(tiles, jnp.where(lane < HEAD_DIM, rotated(tail), tail))


def project_kernel(*refs, chunk_count, first_row):
    chunks = refs[:chunk_count]
    weight_ref, left_q_ref, right_q_ref, cos_ref, sin_ref, out_ref = refs[
        chunk_count : chunk_count + 6
    ]
    token_ref, sems = refs[chunk_count + 6 :]
    chunk_rows = chunks[0].shape[0]
    rows = chunk_rows * chunk_count
    copies = [
        pltpu.make_async_copy(
            chunks[c], token_ref.at[pl.ds(c * chunk_rows, chunk_rows)], sems.at[c]
        )
        for c in range(chunk_count)
    ]
    for copy in copies:
        copy.start()
    for copy in copies:
        copy.wait()
    here = pl.ds(first_row, rows)

    def store(j, value):
        out_ref[j] = value

    project(
        token_ref[...],
        weight_ref,
        left_q_ref[...],
        right_q_ref[...],
        cos_ref[here, :],
        sin_ref[here, :],
        store,
    )


def project_chunks(chunks, first_row, weight, left_q, right_q, cosines, sines):
    chunk_rows, width = chunks[0].shape
    rows = chunk_rows * len(chunks)
    vmem = pl.BlockSpec(memory_space=pltpu.VMEM)
    either = pl.BlockSpec(memory_space=pl.ANY)

    def kernel(*refs):
        project_kernel(*refs, chunk_count=len(chunks), first_row=first_row)

    return pl.pallas_call(
        kernel,
        in_specs=[either] * len(chunks) + [vmem] * 5,
        out_specs=vmem,
        out_shape=jax.ShapeDtypeStruct((weight.shape[1] // LANES, rows, LANES), jnp.float32),
        scratch_shapes=[
            pltpu.VMEM((rows, width), jnp.bfloat16),
            pltpu.SemaphoreType.DMA((len(chunks),)),
        ],
        compiler_params=pltpu.CompilerParams(vmem_limit_bytes=38 * 1024 * 1024),
    )(*chunks, weight, left_q, right_q, cosines, sines)


TOGETHER = 4


def layer_kernel(lengths_ref, sink_ref, place_ref, *refs, chunk_count, ready_count, own_steps):
    chunks = refs[:chunk_count]
    ready = refs[chunk_count : chunk_count + ready_count]
    refs = refs[chunk_count + ready_count :]
    (
        out_weight_hbm,
        key_hbm,
        value_hbm,
        weight_ref,
        left_q_ref,
        right_q_ref,
        left_o_ref,
        right_o_ref,
        cos_ref,
        sin_ref,
    ) = refs[:10]
    (
        token_ref,
        out_weight_ref,
        key_ref,
        value_ref,
        proj_ref,
        att_ref,
        right_ref,
        bias_ref,
        sems,
        chunk_sems,
    ) = refs[-10:]
    outs = refs[10:-10]
    chunk_rows, width = chunks[0].shape
    copies = [
        pltpu.make_async_copy(
            chunks[c], token_ref.at[pl.ds(c * chunk_rows, chunk_rows)], chunk_sems.at[c]
        )
        for c in range(chunk_count)
    ]
    key_copy = pltpu.make_async_copy(key_hbm, key_ref, sems.at[0])
    value_copy = pltpu.make_async_copy(value_hbm, value_ref, sems.at[1])
    out_weight_copy = pltpu.make_async_copy(out_weight_hbm, out_weight_ref, sems.at[2])
    ready_copies = []
    first_row = 0
    for i in range(ready_count):
        count = ready[i].shape[1]
        ready_copies.append(
            pltpu.make_async_copy(
                ready[i], proj_ref.at[:, pl.ds(first_row, count), :], chunk_sems.at[chunk_count + i]
            )
        )
        first_row += count
    for copy in copies + ready_copies + [key_copy, value_copy, out_weight_copy]:
        copy.start()

    seqs = key_ref.shape[0]
    total_rows = proj_ref.shape[1]
    steps = total_rows // seqs
    qdim = right_q_ref.shape[1]
    group = qdim // HEAD_DIM
    tiles = qdim // LANES
    pairs = key_ref.shape[1]
    rows = group * steps

    right_ref[...] = right_rows(right_o_ref[...], noise_scale / math.sqrt(QDIM))
    for copy in copies:
        copy.wait()
    here = pl.ds(first_row, chunk_count * chunk_rows)

    def store(j, value):
        proj_ref[j, here, :] = value

    project(
        token_ref[...],
        weight_ref,
        left_q_ref[...],
        right_q_ref[...],
        cos_ref[here, :],
        sin_ref[here, :],
        store,
    )

    ring = steps // own_steps
    place = place_ref[0]

    def step_of(dim):
        total = jnp.zeros((steps, steps), jnp.int32)
        row = lax.broadcasted_iota(jnp.int32, (steps, steps), dim)
        for order in range(ring):
            distance = (order + 1) // 2
            chunk = (place + ring + (distance if order % 2 else -distance)) & (ring - 1)
            at = order * own_steps
            total = jnp.where(row >= at, chunk * own_steps + row - at, total)
        return total

    bias = jnp.where(step_of(1) <= step_of(0), 0.0, masked_score)
    column = lax.broadcasted_iota(jnp.int32, (steps, LANES - steps), 1)
    for g in range(group):
        bias_ref[g * steps : (g + 1) * steps, :] = jnp.concatenate(
            [bias, jnp.where(column == 0, sink_ref[g], masked_score)], axis=1
        )
    pair = lax.broadcasted_iota(jnp.int32, (1, pairs), 1)
    low_lanes = lax.broadcasted_iota(jnp.int32, (steps, LANES), 1) < HEAD_DIM

    def several(i, carry):
        members = [i * TOGETHER + u for u in range(TOGETHER)]
        evens, odds, news, scored = [], [], [], []
        for b in members:
            even, odd = [], []
            for j in range(tiles):
                t = proj_ref[j, pl.ds(b, steps, stride=seqs), :]
                r = pltpu.roll(t, HEAD_DIM, 1)
                even += [jnp.where(low_lanes, t, 0.0), jnp.where(low_lanes, r, 0.0)]
                odd += [jnp.where(low_lanes, 0.0, r), jnp.where(low_lanes, 0.0, t)]
            evens.append(jnp.concatenate(even, axis=0).astype(jnp.bfloat16))
            odds.append(jnp.concatenate(odd, axis=0).astype(jnp.bfloat16))
            new_pair = proj_ref[tiles, pl.ds(b, steps, stride=seqs), :]
            nothing = jnp.zeros((LANES - steps, LANES), jnp.float32)
            news.append(jnp.concatenate([new_pair, nothing], axis=0).astype(jnp.bfloat16))
        for u, b in enumerate(members):
            length = lengths_ref[b]
            keys = key_ref[b]

            def scores(query, parity):
                valid = jnp.where(2 * pair + parity < length, 0.0, masked_score)
                return (
                    lax.dot_general(
                        query, keys, CONTRACT_LAST, preferred_element_type=jnp.float32
                    )
                    + valid
                )

            s_new = (
                lax.dot_general(
                    evens[u], news[u], CONTRACT_LAST, preferred_element_type=jnp.float32
                )
                + bias_ref[...]
            )
            scored.append((scores(evens[u], 0), scores(odds[u], 1), s_new))
        for u, b in enumerate(members):
            s_even, s_odd, s_new = scored[u]
            values = value_ref[b]

            def folded(join, even, odd, new):
                return functools.reduce(
                    join,
                    [x[:, i : i + LANES] for x in (even, odd) for i in range(0, pairs, LANES)],
                    new,
                )

            top = jnp.max(folded(jnp.maximum, s_even, s_odd, s_new), axis=1, keepdims=True)
            p_even = jnp.exp(s_even - top)
            p_odd = jnp.exp(s_odd - top)
            p_new = jnp.exp(s_new - top)
            total = jnp.sum(folded(jnp.add, p_even, p_odd, p_new), axis=1, keepdims=True)
            a_even = jnp.dot(
                p_even.astype(jnp.bfloat16), values, preferred_element_type=jnp.float32
            )
            a_odd = jnp.dot(
                p_odd.astype(jnp.bfloat16), values, preferred_element_type=jnp.float32
            ) + jnp.dot(p_new.astype(jnp.bfloat16), news[u], preferred_element_type=jnp.float32)
            inverse = 1.0 / total
            a_even = a_even * inverse
            a_odd = a_odd * inverse
            for j in range(tiles):
                g = 2 * j
                e0 = a_even[g * steps : (g + 1) * steps]
                o0 = a_odd[g * steps : (g + 1) * steps]
                e1 = a_even[(g + 1) * steps : (g + 2) * steps]
                o1 = a_odd[(g + 1) * steps : (g + 2) * steps]
                tile = jnp.where(
                    low_lanes, e0 + pltpu.roll(o0, HEAD_DIM, 1), o1 + pltpu.roll(e1, HEAD_DIM, 1)
                )
                att_ref[j, pl.ds(b, steps, stride=seqs), :] = tile
        return carry

    for copy in ready_copies + [key_copy, value_copy]:
        copy.wait()
    lax.fori_loop(0, seqs // TOGETHER, several, 0)

    out_weight_copy.wait()
    attended = jnp.concatenate([att_ref[j] for j in range(tiles)], axis=1).astype(jnp.bfloat16)
    low = lax.dot_general(
        attended, left_rows(left_o_ref[...]), CONTRACT_LAST, preferred_element_type=jnp.float32
    )
    low = low_rank_operand(low)
    for at in range(0, width, 768):
        to = min(at + 768, width)
        share = lax.dot_general(
            attended, out_weight_ref[at:to, :], CONTRACT_LAST, preferred_element_type=jnp.float32
        ) + jnp.dot(low, right_ref[:, at:to], preferred_element_type=jnp.float32)
        share = share.astype(jnp.bfloat16)
        part = total_rows // len(outs)
        for c, out in enumerate(outs):
            out[:, at:to] = share[c * part : (c + 1) * part]


def layer(
    lengths, sinks, place, chunks, ready, out_parts, weight, out_weight, keys, values, own_steps, *operands
):
    chunk_rows, width = chunks[0].shape
    rows = sum(r.shape[1] for r in ready) + chunk_rows * len(chunks)
    joined = weight.shape[1]
    qdim = operands[1].shape[1]
    group_rows = rows // values.shape[0] * qdim // HEAD_DIM
    vmem = pl.BlockSpec(memory_space=pltpu.VMEM)
    smem = pl.BlockSpec(memory_space=pltpu.SMEM)
    either = pl.BlockSpec(memory_space=pl.ANY)

    def kernel(*refs):
        layer_kernel(
            *refs, chunk_count=len(chunks), ready_count=len(ready), own_steps=own_steps
        )

    return pl.pallas_call(
        kernel,
        in_specs=[smem] * 3 + [either] * (len(chunks) + len(ready) + 3) + [vmem] * (1 + len(operands)),
        out_specs=[vmem] * out_parts,
        out_shape=[jax.ShapeDtypeStruct((rows // out_parts, width), jnp.bfloat16)] * out_parts,
        scratch_shapes=[
            pltpu.VMEM((chunk_rows * len(chunks), width), jnp.bfloat16),
            pltpu.VMEM(out_weight.shape, jnp.bfloat16),
            pltpu.VMEM(keys.shape, jnp.bfloat16),
            pltpu.VMEM(values.shape, jnp.bfloat16),
            pltpu.VMEM((joined // LANES, rows, LANES), jnp.float32),
            pltpu.VMEM((qdim // LANES, rows, LANES), jnp.float32),
            pltpu.VMEM((LANES, width), jnp.bfloat16),
            pltpu.VMEM((group_rows, LANES), jnp.float32),
            pltpu.SemaphoreType.DMA((3,)),
            pltpu.SemaphoreType.DMA((len(chunks) + len(ready),)),
        ],
        compiler_params=pltpu.CompilerParams(vmem_limit_bytes=38 * 1024 * 1024),
    )(lengths, sinks, place, *chunks, *ready, out_weight, keys, values, weight, *operands)


def shards(
    hidden,
    joined_weight,
    output_weight,
    key_cache,
    value_cache,
    sink_logits,
    lengths,
    query_left,
    query_right,
    output_left,
    output_right,
    fitness,
    query_master,
    query_moment,
    output_master,
    output_moment,
):
    ring = lax.axis_size("head")
    place = lax.axis_index("head")
    right_pairs = [(i, (i + 1) % ring) for i in range(ring)]
    left_pairs = [(i, (i - 1) % ring) for i in range(ring)]

    def to_right(x):
        return lax.ppermute(x, "head", right_pairs)

    def to_left(x):
        return lax.ppermute(x, "head", left_pairs)

    _, own_steps, row_count, width = hidden.shape
    flat_weight = joined_weight[:, 0, :]

    member_count = lax.axis_size("member")
    factors = pack(fitness, query_left[0], output_right[0], query_right[0], output_left[0])
    held = [factors, factors]

    def exchange(distance, after):
        if distance < 1:
            return after
        mine = held[0]
        if held[1] is not held[0]:
            mine = jnp.concatenate(held, axis=0)
        mine, after = lax.optimization_barrier((mine, after))
        pairs = [(i, i ^ distance) for i in range(member_count)]
        held[0], held[1] = mine, lax.ppermute(mine, "member", pairs)
        return after

    offsets = [0]
    for distance in range(1, ring // 2):
        offsets += [distance, -distance]
    offsets.append(ring // 2)
    chunk_ids = jnp.mod(place + jnp.array(offsets, jnp.int32), ring)
    steps = (
        chunk_ids[:, None] * own_steps + jnp.arange(own_steps, dtype=jnp.int32)[None, :]
    ).reshape(-1)
    half_dim = HEAD_DIM // 2
    lane_ids = jnp.arange(LANES, dtype=jnp.int32)
    exponents = (lane_ids % half_dim).astype(jnp.float32) * (-2.0 / HEAD_DIM)
    frequency = jnp.power(jnp.float32(rotary_base), exponents)
    positions = steps[:, None] + lengths[0][None, :]
    angles = positions.astype(jnp.float32)[..., None] * frequency
    sign = jnp.where(lane_ids % HEAD_DIM < half_dim, -1.0, 1.0).astype(jnp.float32)
    cosines = jnp.cos(angles).reshape(-1, LANES)
    sines = (jnp.sin(angles) * sign).reshape(-1, LANES)

    own = hidden[0].reshape(-1, width)
    half = own.shape[0] // 2
    exchange(member_count // 2, ())
    from_left, from_right = [own, to_right(own)], [own, to_left(own)]
    cosines, sines, onward, back = lax.optimization_barrier(
        (cosines, sines, from_left[1], from_right[1])
    )
    from_left.append(to_right(onward))
    from_right.append(to_left(back))
    exchange(member_count // 4, from_left[1])
    cached = lax.optimization_barrier((key_cache, value_cache, onward))
    keys, values = relayout(cached[0][0, 0], cached[1][0, 0])
    own_rows = own.shape[0]
    factor_operands = (flat_weight, query_left[0], query_right[0], cosines, sines)
    for distance in range(3, ring // 2):
        keys, values, onward, back = lax.optimization_barrier(
            (keys, values, from_left[-1], from_right[-1])
        )
        from_left.append(to_right(onward))
        from_right.append(to_left(back))
    near = [own]
    for distance in range(1, ring // 2):
        near += [from_right[distance], from_left[distance]]
    early = ring - 3
    exchange(member_count // 8, from_left[-2])
    first_projected = project_chunks(near[:early], 0, *factor_operands)
    first_projected, onward, back = lax.optimization_barrier(
        (first_projected, from_left[-1][:half], from_right[-1][half:])
    )
    far = [to_right(onward), to_left(back)]
    second_projected = project_chunks(near[early:], early * own_rows, *factor_operands)
    exchange(member_count // 16, from_left[-1])
    held[0], far[0] = lax.optimization_barrier((held[0], far[0]))
    projected = [first_projected, second_projected]
    shares = layer(
        lengths[0],
        sink_logits,
        place.reshape(1).astype(jnp.int32),
        far,
        projected,
        2 * ring,
        flat_weight,
        output_weight.T,
        keys,
        values,
        own_steps,
        query_left[0],
        query_right[0],
        output_left[0],
        output_right[0],
        cosines,
        sines,
    )

    exchange(member_count // 32, shares[0])
    row_share = query_master.shape[0]
    start = query_right.shape[2] + lax.axis_index("member") * row_share
    updated = update(
        start.reshape(1).astype(jnp.int32),
        *held,
        query_right.shape[1],
        member_count,
        query_moment,
        query_master,
        output_moment,
        output_master,
    )

    at = {
        (offset, k): shares[2 * i + k] for i, offset in enumerate(offsets) for k in range(2)
    }
    last = ring // 2 - 1
    chains = [
        dict(way=to_right, sign=1, k=0, next=last, moving=at[last + 1, 0]),
        dict(way=to_left, sign=-1, k=1, next=last, moving=at[last + 1, 1]),
        dict(way=to_left, sign=-1, k=0, next=last - 1, moving=at[-last, 0]),
        dict(way=to_right, sign=1, k=1, next=last - 1, moving=at[last, 1]),
    ]
    before = None
    for chain in chains:
        chain["moving"] = chain["way"](chain["moving"])
    for _ in range(last):
        for chain in chains:
            if chain["next"] == 0:
                continue
            mine = at[chain["sign"] * chain["next"], chain["k"]]
            if before is not None:
                mine, before = lax.optimization_barrier((mine, before))
            before = (chain["moving"].astype(jnp.float32) + mine.astype(jnp.float32)).astype(
                jnp.bfloat16
            )
            chain["moving"] = chain["way"](before)
            chain["next"] -= 1
    results = [
        (chains[0]["moving"], chains[2]["moving"], at[0, 0]),
        (chains[3]["moving"], chains[1]["moving"], at[0, 1]),
    ]
    mine, updated = lax.optimization_barrier(([r[2] for r in results], tuple(updated)))
    layer_output = []
    for (from_left, from_right, _), own_share in zip(results, mine):
        total = (
            from_left.astype(jnp.float32)
            + from_right.astype(jnp.float32)
            + own_share.astype(jnp.float32)
        )
        layer_output.append(total.astype(jnp.bfloat16).reshape(own_steps // 2, row_count, width))
    layer_output = jnp.concatenate(layer_output, axis=0)[None]
    return (layer_output,) + updated


def solution(mesh):
    placed = (
        P("member", "head", None, None),
        P(None, "head", None),
        P("head", None),
        P("member", "head", None, None),
        P("member", "head", None, None),
        P("head"),
        P("member", None),
        P("member", None, None),
        P("member", None, "head"),
        P("member", None, "head"),
        P("member", None, None),
        P("member"),
        P("member", "head"),
        P("member", "head"),
        P("member", "head"),
        P("member", "head"),
    )
    return jax.shard_map(
        shards,
        mesh=mesh,
        in_specs=placed,
        out_specs=(
            P("member", "head", None, None),
            P("member", "head"),
            P("member", "head"),
            P("member", "head"),
            P("member", "head"),
        ),
        check_vma=False,
    )
```
